256 devices in a mesh: seq: 64 (over z, x_hi, y), tp: 4 (over x_lo, core).
Axes of the slice: x: 4 (x_hi: 2, x_lo: 2; x = x_hi * 2 + x_lo), y: 4, z: 8, core: 2. Of those that a mesh axis runs over, the one named last changes fastest.
Arguments:
- hidden: bfloat16 [16384, 8192], P('seq', 'tp'), may hold values from -6 to 6
- kept_index: int32 [64, 128], P('seq'), may hold values from 0 to 255, as said below
- doc_ids: int32 [16384], P('seq'), may hold values from 0 to 127, never falling along the last dimension, each value on 1 to 512 neighbouring positions
- norm_gain: float32 [8192], replicated, may hold values from 0.5 to 1.5
- w_query: bfloat16 [8192, 4096], P('seq', 'tp'), as said below
- key_value_weight: bfloat16 [8192, 2, 1024], P('seq', None, 'tp'), as said below
Outputs:
- attended: bfloat16 [8192, 4096], P('seq', 'tp')
The draws below stay inside these ranges and needn't reach their ends.
Inputs may be any that keep to these rules, and one draw needn't show every extreme that they name: `kept_index`: each row lists 128 distinct positions of its span in increasing order, always with the span's first and last token. `w_query`: a projection matrix. `key_value_weight`: a projection matrix.
All inputs are finite; a program needn't handle non-finite values.
Results may differ from the reference program's by a relative error of at most 0.0075.
Values may be sent and summed in bfloat16 or wider, within the bound.
A program may use at most 128 MiB of HBM per device.

```python
import math
import jax
import jax.numpy as jnp
import numpy as np
from jax import lax

MODEL_WIDTH = 8192
QUERY_HEADS = 32
KEY_VALUE_HEADS = 8
HEAD_WIDTH = 128
SPAN = 256
KEPT = 128
SPANS = 64
TOKENS = 16384
DOCS = 128


def shared_keys(key):
    return jnp.clip(jax.random.normal(key, (MODEL_WIDTH, 2, KEY_VALUE_HEADS * HEAD_WIDTH), jnp.float32), -6.0, 6.0) * MODEL_WIDTH ** (-0.5)


def draw_key_value_weight(key, part):
    shared_rows = shared_keys(key)
    return shared_rows.astype(jnp.bfloat16)


def draw_w_query(key, part):
    key = jax.random.fold_in(key, 7)
    base = jnp.clip(jax.random.normal(key, (MODEL_WIDTH, QUERY_HEADS * HEAD_WIDTH), jnp.float32), -6.0, 6.0) * MODEL_WIDTH ** (-0.5)
    return base.astype(jnp.bfloat16)


def draw_kept_index(key, part):
    key = jax.random.fold_in(key, 11)
    keys = jax.random.split(key, SPANS)

    def one_span(span_key):
        inner = jax.random.permutation(span_key, SPAN - 2)[:KEPT - 2].astype(jnp.int32) + 1
        full = jnp.concatenate([jnp.zeros((1,), jnp.int32), inner, jnp.full((1,), SPAN - 1, jnp.int32)])
        return jnp.sort(full)
    return jax.vmap(one_span)(keys).astype(jnp.int32)


def steps_of(key, extent, pieces, least, high):
    loudness = 1.0
    for position, shards_of in pieces:
        steps = jax.random.uniform(jax.random.fold_in(jax.random.fold_in(key, 6), position), (shards_of,), jnp.float32, least / len(pieces), high / len(pieces))
        loudness = loudness * jnp.repeat(jnp.exp(steps), extent[position] // shards_of).reshape((-1,) + (1,) * (len(extent) - 1 - position))
    return loudness


def length_profile(amount, total, reach, slope):
    loads = [(1 << 20) // math.isqrt(grade ** slope) + 1 for grade in range(2, amount + 1)]
    surplus, counts = total - reach - (amount - 1), [1] * (amount - 1)
    while surplus > 0:
        free = [i for i in range(amount - 1) if counts[i] < reach]
        mass, left = sum([loads[i] for i in free]), surplus
        for i in free:
            addition = min(reach - counts[i], max(1, left * loads[i] // mass), surplus)
            counts[i] = counts[i] + addition
            surplus = surplus - addition
    return np.array([reach] + counts)


def uneven(own_key, amount, total, most, skew):
    if amount == 2:
        one = jax.random.randint(own_key, (), max(1, total - most), min(most, total - 1) + 1)
        return jnp.stack([one, total - one])
    lengths = jnp.asarray(length_profile(amount, total, most, skew), jnp.int32)
    twos = (amount - 1) // 2
    donor, sink = lengths[1:1 + 2 * twos:2], lengths[2:2 + 2 * twos:2]
    margin = jnp.minimum(donor - 1, most - sink)
    passed = jax.random.randint(jax.random.fold_in(own_key, 1), (twos,), 0, 1 << 20) % (margin + 1)
    lengths = lengths.at[1:1 + 2 * twos:2].set(donor - passed).at[2:2 + 2 * twos:2].set(sink + passed)
    return lengths[jax.random.permutation(jax.random.fold_in(own_key, 2), amount)]


def scatter_about(stream_key, dims, spread, reach, shards=(), held_as=jnp.bfloat16):
    entries = spread * jax.random.normal(stream_key, dims, jnp.float32)
    if shards:
        entries = entries * steps_of(stream_key, dims, shards, -0.22, 0.18)
    return jnp.clip(entries, -reach, reach).astype(held_as)


def setup_inputs(seed: int = 0) -> dict:
    key_list = jax.random.split(jax.random.key(seed), 7)
    return {
        "hidden": scatter_about(key_list[0], (TOKENS, MODEL_WIDTH), 1.0, 6.0, ((0, 64), (1, 4))),
        "kept_index": draw_kept_index(jax.random.fold_in(key_list[6], 71), 0),
        "doc_ids": jnp.searchsorted(jnp.cumsum(uneven(key_list[2], DOCS, TOKENS, 2 * SPAN, 2)), jnp.arange(TOKENS), side="right").astype(jnp.int32),
        "norm_gain": jnp.clip(jax.random.uniform(key_list[3], (MODEL_WIDTH,), jnp.float32, 0.5, 1.5), 0.5, 1.5),
        "w_query": draw_w_query(jax.random.fold_in(key_list[6], 71), 0),
        "key_value_weight": draw_key_value_weight(jax.random.fold_in(key_list[6], 71), 0),
    }


norm_eps = 1e-05
rope_base = 10000.0

def rms_normed(rows, gain):
    values = rows.astype(jnp.float32)
    mean_square = lax.optimization_barrier(jnp.mean(values * values, axis=1, keepdims=True))
    return (values * lax.rsqrt(mean_square + norm_eps) * gain).astype(jnp.bfloat16)

def rotate(values, positions):
    half = values.shape[-1] // 2
    freqs = rope_base ** (-(jnp.arange(half, dtype=jnp.float32) * 2.0) / values.shape[-1])
    angles = positions.astype(jnp.float32)[:, None] * freqs[None, :]
    cosine = jnp.cos(angles)[:, None, :]
    sine = jnp.sin(angles)[:, None, :]
    first = values[..., :half]
    second = values[..., half:]
    return jnp.concatenate([first * cosine - second * sine, second * cosine + first * sine], axis=-1)

def reference(hidden, kept_index, doc_ids, norm_gain, w_query, key_value_weight):
    spans = kept_index.shape[0]
    kept_tokens = kept_index.shape[1]
    span = hidden.shape[0] // spans
    span_width = hidden.shape[1]
    pair_hidden = hidden.reshape(spans // 2, 2, span, span_width)
    pair_kept = kept_index.reshape(spans // 2, 2, kept_tokens)
    pair_docs = doc_ids.reshape(spans // 2, 2, span)
    key_value_flat = key_value_weight.reshape(span_width, 2 * KEY_VALUE_HEADS * HEAD_WIDTH)
    query_group = QUERY_HEADS // KEY_VALUE_HEADS

    def one_pair(items):
        rows, picks, docs = items
        selected = jnp.take_along_axis(rows, picks[:, :, None], axis=1).reshape(2 * kept_tokens, span_width)
        positions = (picks + (jnp.arange(2, dtype=jnp.int32) * span)[:, None]).astype(jnp.int32).reshape(2 * kept_tokens)
        owners = jnp.take_along_axis(docs, picks, axis=1).reshape(2 * kept_tokens)
        normed_hidden = rms_normed(selected, norm_gain)
        query = jnp.dot(normed_hidden, w_query, preferred_element_type=jnp.float32).reshape(2 * kept_tokens, QUERY_HEADS, HEAD_WIDTH)
        key_value_rows = jnp.dot(normed_hidden, key_value_flat, preferred_element_type=jnp.float32).reshape(2 * kept_tokens, 2, KEY_VALUE_HEADS, HEAD_WIDTH)
        rot_query = rotate(query, positions).astype(jnp.bfloat16)
        rot_key = rotate(key_value_rows[:, 0], positions).astype(jnp.bfloat16)
        value = key_value_rows[:, 1].astype(jnp.bfloat16)
        keys = jnp.repeat(rot_key, query_group, axis=1).astype(jnp.float32)
        values = jnp.repeat(value, query_group, axis=1).astype(jnp.float32)
        scores = jnp.einsum('qhd,khd->hqk', rot_query.astype(jnp.float32), keys) * HEAD_WIDTH ** (-0.5)
        allowed = (positions[None, :] <= positions[:, None]) & (owners[None, :] == owners[:, None])
        scores = jnp.where(allowed[None], scores, -1e+30)
        top = lax.optimization_barrier(jnp.max(scores, axis=-1, keepdims=True))
        expo = jnp.exp(scores - top)
        probs = (expo / lax.optimization_barrier(jnp.sum(expo, axis=-1, keepdims=True))).astype(jnp.bfloat16)
        mixed = jnp.einsum('hqk,khd->qhd', probs.astype(jnp.float32), values)
        return mixed.astype(jnp.bfloat16).reshape(2 * kept_tokens, QUERY_HEADS * HEAD_WIDTH)
    out = lax.map(one_pair, (pair_hidden, pair_kept, pair_docs))
    return out.reshape(spans * kept_tokens, QUERY_HEADS * HEAD_WIDTH)
```

```python
import functools
import math

import jax
import jax.numpy as jnp
from jax import lax
from jax.experimental import pallas as pl
from jax.experimental.pallas import tpu as pltpu
from jax.sharding import PartitionSpec as P

MESH = pl.DeviceIdType.MESH
HEAD = 128
KEPT = 128
SPAN = 256
WIDTH = 8192
QUARTER = 2048
CHUNK = 256
CHUNKS = 6
norm_eps = 1e-05
rope_base = 10000.0

GROUPS = ((0, 1, 2), (3, 4, 5))


def kernel(
    hidden, kept, docs, gain_all, wq, wkv, out,
    gain, asrc, abuf, wbuf, pbuf, rbuf, ssb, pdb, kvb, rots,
    gain_sem, w_send, w_recv, a_send, a_recv, f_send, f_recv, p_send, p_recv,
    s_send, s_recv, d_send, d_recv, k_send, k_recv,
):
    f32, bf16 = jnp.float32, jnp.bfloat16
    s = lax.axis_index("seq")
    t = lax.axis_index("tp")
    z, xh, y = s // 8, lax.rem(s // 4, 2), lax.rem(s, 4)
    xl, c = t // 2, lax.rem(t, 2)
    x = xh * 2 + xl
    place = xh * 4 + y
    side = lax.rem(s, 2)

    def at(zz, xx, yy, cc):
        return (zz * 8 + (xx // 2) * 4 + yy, lax.rem(xx, 2) * 2 + cc)

    def plane(dx, dy):
        return lax.rem(x + dx + 4, 4), lax.rem(y + dy + 4, 4)

    up = (lax.rem(s + 8, 64), t)
    down = (lax.rem(s + 56, 64), t)
    sibling = (s, xl * 2 + (1 - c))
    partner = (s + 1 - 2 * side, t)
    moves = [(dx, dy) for dx in range(4) for dy in range(4) if (dx, dy) != (0, 0)]

    gain_copy = pltpu.make_async_copy(gain_all.at[pl.ds(t * 16, 16)], gain, gain_sem)
    gain_copy.start()

    barrier = pltpu.get_barrier_semaphore()

    def greet(device):
        pl.semaphore_signal(barrier, inc=1, device_id=device, device_id_type=MESH)

    greet(up)
    greet(down)
    for dx, dy in moves:
        xx, yy = plane(dx, dy)
        greet(at(z, xx, yy, c))
    greet(sibling)
    greet((s, (1 - xl) * 2 + (1 - c)))

    wbuf[0, z] = wkv[:, 0:CHUNK]
    wbuf[1, z] = wkv[:, CHUNK : 2 * CHUNK]
    for n in range(2, CHUNKS):
        wbuf[n, z] = wq[:, (n - 2) * CHUNK : (n - 1) * CHUNK]

    lane = lax.broadcasted_iota(jnp.int32, (KEPT, KEPT), 1)
    eye = lax.broadcasted_iota(jnp.int32, (KEPT, KEPT), 0) == lane

    def to_column(row):
        return jnp.sum(jnp.where(eye, jnp.broadcast_to(row, (KEPT, KEPT)), 0.0), axis=1, keepdims=True)

    def to_row(column):
        return jnp.sum(jnp.where(eye, jnp.broadcast_to(column, (KEPT, KEPT)), 0.0), axis=0, keepdims=True)

    kept_row = kept[...].astype(f32)
    kept_col = to_column(kept_row)
    columns = lax.broadcasted_iota(jnp.int32, (KEPT, SPAN), 1).astype(f32)
    picks = columns == kept_col
    chosen = jnp.where(picks, 1.0, 0.0).astype(bf16)
    doc_col = jnp.sum(jnp.where(picks, docs[...].astype(f32), 0.0), axis=1, keepdims=True)
    pos_row = kept_row + (side * SPAN).astype(f32)
    pos_col = kept_col + (side * SPAN).astype(f32)
    pdb[side, 0:1, :] = pos_row
    pdb[side, 1:2, :] = to_row(doc_col)

    gain_copy.wait()
    square = jnp.zeros((KEPT, 1), f32)
    for j in range(QUARTER // 256):
        rows = jnp.dot(chosen, hidden[:, j * 256 : (j + 1) * 256], preferred_element_type=f32)
        square += jnp.sum(rows * rows, axis=1, keepdims=True)
        for b in range(2):
            block = 2 * j + b
            scaled = rows[:, b * 128 : (b + 1) * 128] * gain[block : block + 1, :]
            high, to = block // 8, block % 8
            asrc[to, :, high * 128 : (high + 1) * 128] = scaled.astype(bf16)
    ssb[t, 0:1, :] = to_row(square)
    abuf[t, place] = asrc[place]

    pl.semaphore_wait(barrier, 19)

    def remote(src, dst, send, recv, device):
        return pltpu.make_async_remote_copy(
            src_ref=src, dst_ref=dst, send_sem=send, recv_sem=recv, device_id=device, device_id_type=MESH
        )

    sent = []

    def hops(n, way):
        return 4 if (n + way) % 2 == 0 else 3

    def w_copy(n, way, hop):
        origin = lax.rem(z + 8 - (hop - 1), 8) if way == 0 else lax.rem(z + hop - 1, 8)
        slot = wbuf.at[n, origin]
        return remote(slot, slot, w_send.at[n, way, hop - 1], w_recv.at[n, way, hop - 1], up if way == 0 else down)

    def w_arrived(n, way, hop):
        origin = lax.rem(z + 8 - hop, 8) if way == 0 else lax.rem(z + hop, 8)
        slot = wbuf.at[n, origin]
        remote(slot, slot, w_send.at[n, way, hop - 1], w_recv.at[n, way, hop - 1], up if way == 0 else down).wait_recv()

    def w_start(n, hop):
        for way in range(2):
            if hop <= hops(n, way):
                copy = w_copy(n, way, hop)
                copy.start()
                sent.append(copy)

    def w_wait(n, hop):
        for way in range(2):
            if hop <= hops(n, way):
                w_arrived(n, way, hop)

    def w_pass(n, hop):
        for way in range(2):
            if hop <= hops(n, way):
                w_arrived(n, way, hop)
                if hop + 1 <= hops(n, way):
                    copy = w_copy(n, way, hop + 1)
                    copy.start()
                    sent.append(copy)

    for n in GROUPS[0]:
        w_start(n, 1)

    a_copies = []
    for k, (dx, dy) in enumerate(moves):
        xx, yy = plane(dx, dy)
        copy = remote(asrc.at[(xx // 2) * 4 + yy], abuf.at[t, place], a_send.at[k], a_recv.at[k], at(z, xx, yy, c))
        copy.start()
        sent.append(copy)
    for k in range(1, 4):
        copy = remote(ssb.at[t], ssb.at[t], s_send.at[k - 1], s_recv.at[k - 1], (s, lax.rem(t + k, 4)))
        copy.start()
        sent.append(copy)
    copy = remote(pdb.at[side], pdb.at[side], d_send, d_recv, partner)
    copy.start()
    sent.append(copy)

    freqs = jnp.exp(lax.rem(lane, 64).astype(f32) * (-2.0 * math.log(rope_base) / HEAD))
    angles = pos_col * freqs
    rots[0] = jnp.cos(angles)
    sine = jnp.sin(angles)
    rots[1] = jnp.where(lane < 64, -sine, sine)

    for hop in range(1, 4):
        for n in GROUPS[0]:
            w_pass(n, hop)

    f_copies = []
    for dx in range(4):
        for dy in range(4):
            if (dx, dy) == (0, 0):
                continue
            k = moves.index((dx, dy))
            xx, yy = plane(-dx, -dy)
            slot = abuf.at[lax.rem(xx, 2) * 2 + c, (xx // 2) * 4 + yy]
            remote(slot, slot, a_send.at[k], a_recv.at[k], at(z, xx, yy, c)).wait_recv()
        xx, _ = plane(-dx, 0)
        block = abuf.at[lax.rem(xx, 2) * 2 + c, pl.ds((xx // 2) * 4, 4)]
        copy = remote(block, block, f_send.at[dx], f_recv.at[dx], sibling)
        copy.start()
        sent.append(copy)
    for n in GROUPS[1]:
        w_start(n, 1)
    for dx in range(4):
        xx, _ = plane(-dx, 0)
        block = abuf.at[lax.rem(xx, 2) * 2 + (1 - c), pl.ds((xx // 2) * 4, 4)]
        remote(block, block, f_send.at[dx], f_recv.at[dx], sibling).wait_recv()

    def product(n):
        def half(r):
            total = jnp.zeros((512, CHUNK), f32)
            for q in range(4):
                total += jnp.dot(
                    abuf[q, pl.ds(r * 4, 4)].reshape(512, 256),
                    wbuf[n, 2 * q : 2 * q + 2].reshape(256, CHUNK),
                    preferred_element_type=f32,
                )
            pbuf[n, pl.ds(r * 4, 4)] = total.astype(bf16).reshape(4, KEPT, CHUNK)

        pl.loop(0, 2)(half)
        for k in range(1, 8):
            xx, yy = lax.rem(x + 2 * (k // 4), 4), lax.rem(y + k % 4, 4)
            copy = remote(
                pbuf.at[n, (xx // 2) * 4 + yy], rbuf.at[n, k - 1], p_send.at[n, k - 1], p_recv.at[n, k - 1],
                at(z, xx, yy, c),
            )
            copy.start()
            sent.append(copy)

    def summed(n):
        total = pbuf[n, place].astype(f32)
        for k in range(1, 8):
            slot = rbuf.at[n, k - 1]
            remote(slot, slot, p_send.at[n, k - 1], p_recv.at[n, k - 1], sibling).wait_recv()
            total += rbuf[n, k - 1].astype(f32)
        return total * scale

    def rotated(block):
        heads = []
        for h in range(2):
            head = block[:, h * HEAD : (h + 1) * HEAD]
            heads.append((head * rots[0] + pltpu.roll(head, 64, 1) * rots[1]).astype(bf16))
        return heads

    for n in GROUPS[0]:
        w_wait(n, 4)
        product(n)

    for k in range(1, 4):
        slot = ssb.at[lax.rem(t + 4 - k, 4)]
        remote(slot, slot, s_send.at[k - 1], s_recv.at[k - 1], sibling).wait_recv()
    squares = ssb[0, 0:1, :] + ssb[1, 0:1, :] + ssb[2, 0:1, :] + ssb[3, 0:1, :]
    scale = lax.rsqrt(to_column(squares) * (1.0 / WIDTH) + norm_eps)

    slot = pdb.at[1 - side]
    remote(slot, slot, d_send, d_recv, partner).wait_recv()
    key_pos = jnp.concatenate([pdb[0, 0:1, :], pdb[1, 0:1, :]], axis=1)
    key_doc = jnp.concatenate([pdb[0, 1:2, :], pdb[1, 1:2, :]], axis=1)
    allowed = (key_pos <= pos_col) & (key_doc == doc_col)

    def share(j):
        rows = kvb.at[j, side]
        copy = remote(rows, rows, k_send.at[j], k_recv.at[j], partner)
        copy.start()
        sent.append(copy)

    def keys():
        first, second = rotated(summed(0))
        kvb[0, side, :, 0:HEAD] = first
        kvb[0, side, :, HEAD : 2 * HEAD] = second
        share(0)

    def values():
        kvb[1, side] = summed(1).astype(bf16)
        share(1)

    def attend(n):
        head = (n - 2) // 2
        queries = rotated(summed(n))
        key = kvb[0, :, :, head * HEAD : (head + 1) * HEAD].reshape(2 * KEPT, HEAD)
        value = kvb[1, :, :, head * HEAD : (head + 1) * HEAD].reshape(2 * KEPT, HEAD)
        for h in range(2):
            score = lax.dot_general(
                queries[h], key, (((1,), (1,)), ((), ())), preferred_element_type=f32
            ) * (HEAD ** -0.5)
            score = jnp.where(allowed, score, -1e30)
            top = jnp.max(score, axis=1, keepdims=True)
            expo = jnp.exp(score - top)
            norm = jnp.sum(expo, axis=1, keepdims=True)
            mixed = jnp.dot(expo.astype(bf16), value, preferred_element_type=f32) / norm
            place_at = ((n - 2) * 2 + h) * HEAD
            out[:, place_at : place_at + HEAD] = mixed.astype(bf16)

    for n in GROUPS[1]:
        w_pass(n, 1)
    keys()
    for n in GROUPS[1]:
        w_pass(n, 2)
    values()
    for n in GROUPS[1]:
        w_pass(n, 3)
    for n in GROUPS[1]:
        w_wait(n, 4)
        product(n)
    for j in range(2):
        slot = kvb.at[j, 1 - side]
        remote(slot, slot, k_send.at[j], k_recv.at[j], partner).wait_recv()
    for n in range(2, CHUNKS):
        attend(n)
    for copy in sent:
        copy.wait_send()


def body(hidden, kept_index, doc_ids, norm_gain, w_query, key_value_weight):
    f32, bf16 = jnp.float32, jnp.bfloat16
    dma = pltpu.SemaphoreType.DMA
    vmem = pl.BlockSpec(memory_space=pltpu.VMEM)
    return pl.pallas_call(
        kernel,
        out_shape=jax.ShapeDtypeStruct((KEPT, 1024), bf16),
        in_specs=[vmem, vmem, vmem, pl.BlockSpec(memory_space=pl.ANY), vmem, vmem],
        out_specs=vmem,
        scratch_shapes=[
            pltpu.VMEM((16, 128), f32),
            pltpu.VMEM((8, KEPT, 256), bf16),
            pltpu.VMEM((4, 8, KEPT, 256), bf16),
            pltpu.VMEM((CHUNKS, 8, 128, CHUNK), bf16),
            pltpu.VMEM((CHUNKS, 8, KEPT, CHUNK), bf16),
            pltpu.VMEM((CHUNKS, 7, KEPT, CHUNK), bf16),
            pltpu.VMEM((4, 8, 128), f32),
            pltpu.VMEM((2, 8, 128), f32),
            pltpu.VMEM((2, 2, KEPT, 256), bf16),
            pltpu.VMEM((2, KEPT, HEAD), f32),
            dma,
            dma((CHUNKS, 2, 4)), dma((CHUNKS, 2, 4)),
            dma((15,)), dma((15,)),
            dma((4,)), dma((4,)),
            dma((CHUNKS, 7)), dma((CHUNKS, 7)),
            dma((3,)), dma((3,)),
            dma, dma,
            dma((2,)), dma((2,)),
        ],
        compiler_params=pltpu.CompilerParams(
            collective_id=0, has_side_effects=True, vmem_limit_bytes=48 * 1024 * 1024
        ),
    )(
        hidden, kept_index, doc_ids.reshape(1, SPAN), norm_gain.reshape(WIDTH // 128, 128),
        w_query, key_value_weight.reshape(128, 512),
    )


def solution(mesh):
    placed = (P("seq", "tp"), P("seq", None), P("seq"), P(), P("seq", "tp"), P("seq", None, "tp"))
    return jax.shard_map(
        body, mesh=mesh, in_specs=placed, out_specs=P("seq", "tp"), check_vma=False
    )
```

```python
import functools
import math

import jax
import jax.numpy as jnp
from jax import lax
from jax.experimental import pallas as pl
from jax.experimental.pallas import tpu as pltpu
from jax.sharding import PartitionSpec as P

MESH = pl.DeviceIdType.MESH
HEAD = 128
KEPT = 128
SPAN = 256
WIDTH = 8192
QUARTER = 2048
CHUNK = 256
CHUNKS = 6
norm_eps = 1e-05
rope_base = 10000.0

GROUPS = ((0, 1, 2), (3, 4, 5))
X_FIRST = (True, False, True, False, True, False)


def kernel(
    hidden_in, kept_in, docs_in, gain_in, wq, wkv_in, out,
    hidden, kept, docs, gain, wkv, asrc, abuf, wbuf, pbuf, qbuf, rbuf, ssb, pdb, kvb, rots,
    load_sem, w_send, w_recv, a_send, a_recv, f_send, f_recv, p_send, p_recv,
    s_send, s_recv, d_send, d_recv, k_send, k_recv,
):
    f32, bf16 = jnp.float32, jnp.bfloat16
    s = lax.axis_index("seq")
    t = lax.axis_index("tp")
    z, xh, y = s // 8, lax.rem(s // 4, 2), lax.rem(s, 4)
    xl, c = t // 2, lax.rem(t, 2)
    x = xh * 2 + xl
    place = xh * 4 + y
    side = lax.rem(s, 2)

    def at(zz, xx, yy, cc):
        return (zz * 8 + (xx // 2) * 4 + yy, lax.rem(xx, 2) * 2 + cc)

    def plane(dx, dy):
        return lax.rem(x + dx + 4, 4), lax.rem(y + dy + 4, 4)

    up = (lax.rem(s + 8, 64), t)
    down = (lax.rem(s + 56, 64), t)
    sibling = (s, xl * 2 + (1 - c))
    partner = (s + 1 - 2 * side, t)
    moves = [(dx, dy) for dx in range(4) for dy in range(4) if (dx, dy) != (0, 0)]

    barrier = pltpu.get_barrier_semaphore()

    def greet(device):
        pl.semaphore_signal(barrier, inc=1, device_id=device, device_id_type=MESH)

    greet(up)
    greet(down)
    for dx, dy in moves:
        xx, yy = plane(dx, dy)
        greet(at(z, xx, yy, c))
    greet(sibling)
    greet((s, (1 - xl) * 2 + (1 - c)))

    loads = [
        pltpu.make_async_copy(src, dst, load_sem.at[i])
        for i, (src, dst) in enumerate(
            [
                (kept_in, kept),
                (docs_in, docs),
                (hidden_in, hidden),
                (gain_in.at[pl.ds(t * 16, 16)], gain),
                (wkv_in, wkv),
            ]
            + [(wq.at[:, pl.ds(n * CHUNK, CHUNK)], wbuf.at[n + 2, z]) for n in range(4)]
        )
    ]
    for load in loads:
        load.start()

    lane = lax.broadcasted_iota(jnp.int32, (KEPT, KEPT), 1)
    eye = lax.broadcasted_iota(jnp.int32, (KEPT, KEPT), 0) == lane

    def to_column(row):
        return jnp.sum(jnp.where(eye, jnp.broadcast_to(row, (KEPT, KEPT)), 0.0), axis=1, keepdims=True)

    def to_row(column):
        return jnp.sum(jnp.where(eye, jnp.broadcast_to(column, (KEPT, KEPT)), 0.0), axis=0, keepdims=True)

    loads[0].wait()
    loads[1].wait()
    kept_row = kept[...].astype(f32)
    kept_col = to_column(kept_row)
    columns = lax.broadcasted_iota(jnp.int32, (KEPT, SPAN), 1).astype(f32)
    picks = columns == kept_col
    chosen = jnp.where(picks, 1.0, 0.0).astype(bf16)
    doc_col = jnp.sum(jnp.where(picks, docs[...].astype(f32), 0.0), axis=1, keepdims=True)
    pos_row = kept_row + (side * SPAN).astype(f32)
    pos_col = kept_col + (side * SPAN).astype(f32)
    pdb[side, 0:1, :] = pos_row
    pdb[side, 1:2, :] = to_row(doc_col)

    loads[2].wait()
    loads[3].wait()
    square = jnp.zeros((KEPT, 1), f32)
    for j in range(QUARTER // 256):
        rows = jnp.dot(chosen, hidden[:, j * 256 : (j + 1) * 256], preferred_element_type=f32)
        square += jnp.sum(rows * rows, axis=1, keepdims=True)
        for b in range(2):
            block = 2 * j + b
            scaled = rows[:, b * 128 : (b + 1) * 128] * gain[block : block + 1, :]
            high, to = block // 8, block % 8
            asrc[to, :, high * 128 : (high + 1) * 128] = scaled.astype(bf16)
    ssb[t, 0:1, :] = to_row(square)
    abuf[t, place] = asrc[place]
    for load in loads[4:]:
        load.wait()
    wbuf[0, z] = wkv[:, 0, :]
    wbuf[1, z] = wkv[:, 1, :]

    pl.semaphore_wait(barrier, 19)

    def remote(src, dst, send, recv, device):
        return pltpu.make_async_remote_copy(
            src_ref=src, dst_ref=dst, send_sem=send, recv_sem=recv, device_id=device, device_id_type=MESH
        )

    sent = []

    def hops(n, way):
        return 4 if (n + way) % 2 == 0 else 3

    def w_copy(n, way, hop):
        origin = lax.rem(z + 8 - (hop - 1), 8) if way == 0 else lax.rem(z + hop - 1, 8)
        slot = wbuf.at[n, origin]
        return remote(slot, slot, w_send.at[n, way, hop - 1], w_recv.at[n, way, hop - 1], up if way == 0 else down)

    def w_arrived(n, way, hop):
        origin = lax.rem(z + 8 - hop, 8) if way == 0 else lax.rem(z + hop, 8)
        slot = wbuf.at[n, origin]
        remote(slot, slot, w_send.at[n, way, hop - 1], w_recv.at[n, way, hop - 1], up if way == 0 else down).wait_recv()

    def w_start(n, hop):
        for way in range(2):
            if hop <= hops(n, way):
                copy = w_copy(n, way, hop)
                copy.start()
                sent.append(copy)

    def w_wait(n, hop):
        for way in range(2):
            if hop <= hops(n, way):
                w_arrived(n, way, hop)

    def w_pass(n, hop):
        for way in range(2):
            if hop <= hops(n, way):
                w_arrived(n, way, hop)
                if hop + 1 <= hops(n, way):
                    copy = w_copy(n, way, hop + 1)
                    copy.start()
                    sent.append(copy)

    for n in GROUPS[0]:
        w_start(n, 1)

    for k, (dx, dy) in enumerate(moves):
        xx, yy = plane(dx, dy)
        copy = remote(asrc.at[(xx // 2) * 4 + yy], abuf.at[t, place], a_send.at[k], a_recv.at[k], at(z, xx, yy, c))
        copy.start()
        sent.append(copy)
    for k in range(1, 4):
        copy = remote(ssb.at[t], ssb.at[t], s_send.at[k - 1], s_recv.at[k - 1], (s, lax.rem(t + k, 4)))
        copy.start()
        sent.append(copy)
    copy = remote(pdb.at[side], pdb.at[side], d_send, d_recv, partner)
    copy.start()
    sent.append(copy)

    freqs = jnp.exp(lax.rem(lane, 64).astype(f32) * (-2.0 * math.log(rope_base) / HEAD))
    angles = pos_col * freqs
    rots[0] = jnp.cos(angles)
    sine = jnp.sin(angles)
    rots[1] = jnp.where(lane < 64, -sine, sine)

    for hop in range(1, 4):
        for n in GROUPS[0]:
            w_pass(n, hop)

    for dx in range(4):
        for dy in range(4):
            if (dx, dy) == (0, 0):
                continue
            k = moves.index((dx, dy))
            xx, yy = plane(-dx, -dy)
            slot = abuf.at[lax.rem(xx, 2) * 2 + c, (xx // 2) * 4 + yy]
            remote(slot, slot, a_send.at[k], a_recv.at[k], at(z, xx, yy, c)).wait_recv()
        xx, _ = plane(-dx, 0)
        block = abuf.at[lax.rem(xx, 2) * 2 + c, pl.ds((xx // 2) * 4, 4)]
        copy = remote(block, block, f_send.at[dx], f_recv.at[dx], sibling)
        copy.start()
        sent.append(copy)
    for n in GROUPS[1]:
        w_start(n, 1)
    for dx in range(4):
        xx, _ = plane(-dx, 0)
        block = abuf.at[lax.rem(xx, 2) * 2 + (1 - c), pl.ds((xx // 2) * 4, 4)]
        remote(block, block, f_send.at[dx], f_recv.at[dx], sibling).wait_recv()

    def product(n):
        def half(r):
            total = jnp.zeros((512, CHUNK), f32)
            for q in range(4):
                total += jnp.dot(
                    abuf[q, pl.ds(r * 4, 4)].reshape(512, 256),
                    wbuf[n, 2 * q : 2 * q + 2].reshape(256, CHUNK),
                    preferred_element_type=f32,
                )
            pbuf[n, pl.ds(r * 4, 4)] = total.astype(bf16).reshape(4, KEPT, CHUNK)

        pl.loop(0, 2)(half)
        for slot, block, device in first_step(n):
            copy = remote(pbuf.at[n, block], rbuf.at[n, slot], p_send.at[n, slot], p_recv.at[n, slot], device)
            copy.start()
            sent.append(copy)

    across = at(z, lax.rem(x + 2, 4), y, c)
    far_place = (1 - xh) * 4 + y

    def along(dy):
        return lax.rem(y + dy, 4)

    def first_step(n):
        if X_FIRST[n]:
            return [(dy, (1 - xh) * 4 + along(dy), across) for dy in (2, 1, 3, 0)]
        return [
            (3 * own + dy - 1, (xh if own else 1 - xh) * 4 + along(dy), at(z, x, along(dy), c))
            for own in range(2)
            for dy in (2, 1, 3)
        ]

    def arrived(n, slot):
        ref = rbuf.at[n, slot]
        remote(ref, ref, p_send.at[n, slot], p_recv.at[n, slot], across).wait_recv()
        return rbuf[n, slot].astype(f32)

    def second_step(n):
        if X_FIRST[n]:
            for dy in (2, 1, 3):
                total = pbuf[n, xh * 4 + along(dy)].astype(f32) + arrived(n, dy)
                qbuf[n, dy - 1] = total.astype(bf16)
                copy = remote(
                    qbuf.at[n, dy - 1], rbuf.at[n, 3 + dy], p_send.at[n, 3 + dy], p_recv.at[n, 3 + dy],
                    at(z, x, along(dy), c),
                )
                copy.start()
                sent.append(copy)
        else:
            total = pbuf[n, far_place].astype(f32)
            for dy in (1, 3, 2):
                total += arrived(n, dy - 1)
            qbuf[n, 0] = total.astype(bf16)
            copy = remote(qbuf.at[n, 0], rbuf.at[n, 6], p_send.at[n, 6], p_recv.at[n, 6], across)
            copy.start()
            sent.append(copy)

    def summed(n):
        total = pbuf[n, place].astype(f32)
        for slot in (0, 4, 6, 5) if X_FIRST[n] else (3, 5, 4, 6):
            total += arrived(n, slot)
        return total * scale

    def rotated(block):
        heads = []
        for h in range(2):
            head = block[:, h * HEAD : (h + 1) * HEAD]
            heads.append((head * rots[0] + pltpu.roll(head, 64, 1) * rots[1]).astype(bf16))
        return heads

    for n in GROUPS[0]:
        w_wait(n, 4)
        product(n)

    for k in range(1, 4):
        slot = ssb.at[lax.rem(t + 4 - k, 4)]
        remote(slot, slot, s_send.at[k - 1], s_recv.at[k - 1], sibling).wait_recv()
    squares = ssb[0, 0:1, :] + ssb[1, 0:1, :] + ssb[2, 0:1, :] + ssb[3, 0:1, :]
    scale = lax.rsqrt(to_column(squares) * (1.0 / WIDTH) + norm_eps)

    slot = pdb.at[1 - side]
    remote(slot, slot, d_send, d_recv, partner).wait_recv()
    key_pos = jnp.concatenate([pdb[0, 0:1, :], pdb[1, 0:1, :]], axis=1)
    key_doc = jnp.concatenate([pdb[0, 1:2, :], pdb[1, 1:2, :]], axis=1)
    allowed = (key_pos <= pos_col) & (key_doc == doc_col)

    def share(j):
        rows = kvb.at[j, side]
        copy = remote(rows, rows, k_send.at[j], k_recv.at[j], partner)
        copy.start()
        sent.append(copy)

    def keys():
        first, second = rotated(summed(0))
        kvb[0, side, :, 0:HEAD] = first
        kvb[0, side, :, HEAD : 2 * HEAD] = second
        share(0)

    def values():
        kvb[1, side] = summed(1).astype(bf16)
        share(1)

    def attend(n):
        head = (n - 2) // 2
        queries = rotated(summed(n))
        key = kvb[0, :, :, head * HEAD : (head + 1) * HEAD].reshape(2 * KEPT, HEAD)
        value = kvb[1, :, :, head * HEAD : (head + 1) * HEAD].reshape(2 * KEPT, HEAD)
        for h in range(2):
            score = lax.dot_general(
                queries[h], key, (((1,), (1,)), ((), ())), preferred_element_type=f32
            ) * (HEAD ** -0.5)
            score = jnp.where(allowed, score, -1e30)
            top = jnp.max(score, axis=1, keepdims=True)
            expo = jnp.exp(score - top)
            norm = jnp.sum(expo, axis=1, keepdims=True)
            mixed = jnp.dot(expo.astype(bf16), value, preferred_element_type=f32) / norm
            place_at = ((n - 2) * 2 + h) * HEAD
            out[:, place_at : place_at + HEAD] = mixed.astype(bf16)

    def joined():
        for j in range(2):
            slot = kvb.at[j, 1 - side]
            remote(slot, slot, k_send.at[j], k_recv.at[j], partner).wait_recv()

    for n in GROUPS[1]:
        w_pass(n, 1)
    for n in GROUPS[1]:
        w_pass(n, 2)
    second_step(0)
    second_step(1)
    for n in GROUPS[1]:
        w_pass(n, 3)
    values()
    keys()
    for n in GROUPS[1]:
        w_wait(n, 4)
        product(n)
    second_step(2)
    joined()
    attend(2)
    second_step(3)
    second_step(4)
    attend(3)
    second_step(5)
    attend(4)
    attend(5)
    for copy in sent:
        copy.wait_send()


def body(hidden, kept_index, doc_ids, norm_gain, w_query, key_value_weight):
    f32, bf16 = jnp.float32, jnp.bfloat16
    dma = pltpu.SemaphoreType.DMA
    vmem = pl.BlockSpec(memory_space=pltpu.VMEM)
    return pl.pallas_call(
        kernel,
        out_shape=jax.ShapeDtypeStruct((KEPT, 1024), bf16),
        in_specs=[pl.BlockSpec(memory_space=pl.ANY)] * 6,
        out_specs=vmem,
        scratch_shapes=[
            pltpu.VMEM((SPAN, QUARTER), bf16),
            pltpu.VMEM((1, KEPT), jnp.int32),
            pltpu.VMEM((1, SPAN), jnp.int32),
            pltpu.VMEM((16, 128), f32),
            pltpu.VMEM((128, 2, 256), bf16),
            pltpu.VMEM((8, KEPT, 256), bf16),
            pltpu.VMEM((4, 8, KEPT, 256), bf16),
            pltpu.VMEM((CHUNKS, 8, 128, CHUNK), bf16),
            pltpu.VMEM((CHUNKS, 8, KEPT, CHUNK), bf16),
            pltpu.VMEM((CHUNKS, 3, KEPT, CHUNK), bf16),
            pltpu.VMEM((CHUNKS, 7, KEPT, CHUNK), bf16),
            pltpu.VMEM((4, 8, 128), f32),
            pltpu.VMEM((2, 8, 128), f32),
            pltpu.VMEM((2, 2, KEPT, 256), bf16),
            pltpu.VMEM((2, KEPT, HEAD), f32),
            dma((9,)),
            dma((CHUNKS, 2, 4)), dma((CHUNKS, 2, 4)),
            dma((15,)), dma((15,)),
            dma((4,)), dma((4,)),
            dma((CHUNKS, 7)), dma((CHUNKS, 7)),
            dma((3,)), dma((3,)),
            dma, dma,
            dma((2,)), dma((2,)),
        ],
        compiler_params=pltpu.CompilerParams(
            collective_id=0, has_side_effects=True, vmem_limit_bytes=56 * 1024 * 1024
        ),
    )(
        hidden, kept_index, doc_ids.reshape(1, SPAN), norm_gain.reshape(WIDTH // 128, 128),
        w_query, key_value_weight,
    )


def solution(mesh):
    placed = (P("seq", "tp"), P("seq", None), P("seq"), P(), P("seq", "tp"), P("seq", None, "tp"))
    return jax.shard_map(
        body, mesh=mesh, in_specs=placed, out_specs=P("seq", "tp"), check_vma=False
    )
```

```python
import functools
import math

import jax
import jax.numpy as jnp
from jax import lax
from jax.experimental import pallas as pl
from jax.experimental.pallas import tpu as pltpu
from jax.sharding import PartitionSpec as P

MESH = pl.DeviceIdType.MESH
HEAD = 128
KEPT = 128
SPAN = 256
WIDTH = 8192
QUARTER = 2048
CHUNK = 256
CHUNKS = 6
norm_eps = 1e-05
rope_base = 10000.0

X_FIRST = (False, True, False, True, False, True)


def kernel(
    hidden_in, kept_in, docs_in, gain_in, wq, wkv_in, out,
    hidden, kept, docs, gain, wkv, asrc, abuf, wbuf, pbuf, qbuf, rbuf, ssb, pdb, kvb, rots,
    load_sem, w_send, w_recv, a_send, a_recv, f_send, f_recv, p_send, p_recv,
    s_send, s_recv, d_send, d_recv, k_send, k_recv,
):
    f32, bf16 = jnp.float32, jnp.bfloat16
    s = lax.axis_index("seq")
    t = lax.axis_index("tp")
    z, xh, y = s // 8, lax.rem(s // 4, 2), lax.rem(s, 4)
    xl, c = t // 2, lax.rem(t, 2)
    x = xh * 2 + xl
    place = xh * 4 + y
    side = lax.rem(s, 2)

    def at(zz, xx, yy, cc):
        return (zz * 8 + (xx // 2) * 4 + yy, lax.rem(xx, 2) * 2 + cc)

    def plane(dx, dy):
        return lax.rem(x + dx + 4, 4), lax.rem(y + dy + 4, 4)

    up = (lax.rem(s + 8, 64), t)
    down = (lax.rem(s + 56, 64), t)
    sibling = (s, xl * 2 + (1 - c))
    partner = (s + 1 - 2 * side, t)
    moves = [(dx, dy) for dx in range(4) for dy in range(4) if (dx, dy) != (0, 0)]
    moves.sort(key=lambda m: -min(m[0], 4 - m[0]) - min(m[1], 4 - m[1]))

    barrier = pltpu.get_barrier_semaphore()

    def greet(device):
        pl.semaphore_signal(barrier, inc=1, device_id=device, device_id_type=MESH)

    greet(up)
    greet(down)
    for dx, dy in moves:
        xx, yy = plane(dx, dy)
        greet(at(z, xx, yy, c))
    greet(sibling)
    greet((s, (1 - xl) * 2 + (1 - c)))

    loads = [
        pltpu.make_async_copy(src, dst, load_sem.at[i])
        for i, (src, dst) in enumerate(
            [
                (kept_in, kept),
                (docs_in, docs),
                (hidden_in, hidden),
                (gain_in.at[pl.ds(t * 16, 16)], gain),
                (wkv_in, wkv),
            ]
            + [(wq.at[:, pl.ds(n * CHUNK, CHUNK)], wbuf.at[n + 2, z]) for n in range(4)]
        )
    ]
    for load in loads:
        load.start()

    lane = lax.broadcasted_iota(jnp.int32, (KEPT, KEPT), 1)
    eye = lax.broadcasted_iota(jnp.int32, (KEPT, KEPT), 0) == lane

    def to_column(row):
        return jnp.sum(jnp.where(eye, jnp.broadcast_to(row, (KEPT, KEPT)), 0.0), axis=1, keepdims=True)

    def to_row(column):
        return jnp.sum(jnp.where(eye, jnp.broadcast_to(column, (KEPT, KEPT)), 0.0), axis=0, keepdims=True)

    loads[0].wait()
    loads[1].wait()
    kept_row = kept[...].astype(f32)
    kept_col = to_column(kept_row)
    columns = lax.broadcasted_iota(jnp.int32, (KEPT, SPAN), 1).astype(f32)
    picks = columns == kept_col
    chosen = jnp.where(picks, 1.0, 0.0).astype(bf16)
    doc_col = jnp.sum(jnp.where(picks, docs[...].astype(f32), 0.0), axis=1, keepdims=True)
    pos_row = kept_row + (side * SPAN).astype(f32)
    pos_col = kept_col + (side * SPAN).astype(f32)
    pdb[side, 0:1, :] = pos_row
    pdb[side, 1:2, :] = to_row(doc_col)

    loads[2].wait()
    loads[3].wait()
    square = jnp.zeros((KEPT, 1), f32)
    for j in range(QUARTER // 256):
        rows = jnp.dot(chosen, hidden[:, j * 256 : (j + 1) * 256], preferred_element_type=f32)
        square += jnp.sum(rows * rows, axis=1, keepdims=True)
        for b in range(2):
            block = 2 * j + b
            scaled = rows[:, b * 128 : (b + 1) * 128] * gain[block : block + 1, :]
            high, to = block // 8, block % 8
            asrc[to, :, high * 128 : (high + 1) * 128] = scaled.astype(bf16)
    ssb[t, 0:1, :] = to_row(square)
    abuf[t, place] = asrc[place]
    for load in loads[4:]:
        load.wait()
    wbuf[0, z] = wkv[:, 0, :]
    wbuf[1, z] = wkv[:, 1, :]

    pl.semaphore_wait(barrier, 19)

    def remote(src, dst, send, recv, device):
        return pltpu.make_async_remote_copy(
            src_ref=src, dst_ref=dst, send_sem=send, recv_sem=recv, device_id=device, device_id_type=MESH
        )

    sent = []

    def hops(n, way):
        return 4 if (n + way) % 2 == 0 else 3

    def w_slot(n, way, hop):
        origin = lax.rem(z + 8 - hop, 8) if way == 0 else lax.rem(z + hop, 8)
        return wbuf.at[n, origin]

    def w_send_on(n, way, hop):
        slot = w_slot(n, way, hop - 1)
        copy = remote(slot, slot, w_send.at[n, way, hop - 1], w_recv.at[n, way, hop - 1], down if way else up)
        copy.start()
        sent.append(copy)

    def w_arrived(n, way, hop):
        slot = w_slot(n, way, hop)
        remote(slot, slot, w_send.at[n, way, hop - 1], w_recv.at[n, way, hop - 1], down if way else up).wait_recv()

    def start(n):
        for way in range(2):
            w_send_on(n, way, 1)

    def relay(n, hop, way):
        w_arrived(n, way, hop)
        w_send_on(n, way, hop + 1)

    for n in (0, 1, 2):
        start(n)

    for k, (dx, dy) in enumerate(moves):
        xx, yy = plane(dx, dy)
        copy = remote(asrc.at[(xx // 2) * 4 + yy], abuf.at[t, place], a_send.at[k], a_recv.at[k], at(z, xx, yy, c))
        copy.start()
        sent.append(copy)
    for k in range(1, 4):
        copy = remote(ssb.at[t], ssb.at[t], s_send.at[k - 1], s_recv.at[k - 1], (s, lax.rem(t + k, 4)))
        copy.start()
        sent.append(copy)
    copy = remote(pdb.at[side], pdb.at[side], d_send, d_recv, partner)
    copy.start()
    sent.append(copy)

    freqs = jnp.exp(lax.rem(lane, 64).astype(f32) * (-2.0 * math.log(rope_base) / HEAD))
    angles = pos_col * freqs
    rots[0] = jnp.cos(angles)
    sine = jnp.sin(angles)
    rots[1] = jnp.where(lane < 64, -sine, sine)

    def hand_on(dx):
        for dy in range(4):
            if (dx, dy) == (0, 0):
                continue
            k = moves.index((dx, dy))
            xx, yy = plane(-dx, -dy)
            slot = abuf.at[lax.rem(xx, 2) * 2 + c, (xx // 2) * 4 + yy]
            remote(slot, slot, a_send.at[k], a_recv.at[k], at(z, xx, yy, c)).wait_recv()
        xx, _ = plane(-dx, 0)
        block = abuf.at[lax.rem(xx, 2) * 2 + c, pl.ds((xx // 2) * 4, 4)]
        copy = remote(block, block, f_send.at[dx], f_recv.at[dx], sibling)
        copy.start()
        sent.append(copy)

    def rows_ready():
        for dx in range(4):
            xx, _ = plane(-dx, 0)
            block = abuf.at[lax.rem(xx, 2) * 2 + (1 - c), pl.ds((xx // 2) * 4, 4)]
            remote(block, block, f_send.at[dx], f_recv.at[dx], sibling).wait_recv()

    def product(n):
        for way in range(2):
            w_arrived(n, way, hops(n, way))

        def half(r):
            total = jnp.zeros((512, CHUNK), f32)
            for q in range(4):
                total += jnp.dot(
                    abuf[q, pl.ds(r * 4, 4)].reshape(512, 256),
                    wbuf[n, 2 * q : 2 * q + 2].reshape(256, CHUNK),
                    preferred_element_type=f32,
                )
            pbuf[n, pl.ds(r * 4, 4)] = total.astype(bf16).reshape(4, KEPT, CHUNK)

        pl.loop(0, 2)(half)
        for slot, block, device in first_step(n):
            copy = remote(pbuf.at[n, block], rbuf.at[n, slot], p_send.at[n, slot], p_recv.at[n, slot], device)
            copy.start()
            sent.append(copy)

    across = at(z, lax.rem(x + 2, 4), y, c)
    far_place = (1 - xh) * 4 + y

    def along(dy):
        return lax.rem(y + dy, 4)

    def first_step(n):
        if X_FIRST[n]:
            return [(dy, (1 - xh) * 4 + along(dy), across) for dy in (2, 1, 3, 0)]
        return [
            (3 * own + dy - 1, (xh if own else 1 - xh) * 4 + along(dy), at(z, x, along(dy), c))
            for own in range(2)
            for dy in (2, 1, 3)
        ]

    def arrived(n, slot):
        ref = rbuf.at[n, slot]
        remote(ref, ref, p_send.at[n, slot], p_recv.at[n, slot], across).wait_recv()
        return rbuf[n, slot].astype(f32)

    def second(n, dy):
        if X_FIRST[n]:
            total = pbuf[n, xh * 4 + along(dy)].astype(f32) + arrived(n, dy)
            slot, device = 3 + dy, at(z, x, along(dy), c)
        else:
            total = pbuf[n, far_place].astype(f32)
            for other in range(3):
                total += arrived(n, other)
            slot, device = 6, across
        qbuf[n, slot - 4] = total.astype(bf16)
        copy = remote(qbuf.at[n, slot - 4], rbuf.at[n, slot], p_send.at[n, slot], p_recv.at[n, slot], device)
        copy.start()
        sent.append(copy)

    def summed(n):
        total = pbuf[n, place].astype(f32)
        for slot in (0, 4, 6, 5) if X_FIRST[n] else (3, 5, 4, 6):
            total += arrived(n, slot)
        return total * scales[0]

    def rotated(block):
        heads = []
        for h in range(2):
            head = block[:, h * HEAD : (h + 1) * HEAD]
            heads.append((head * rots[0] + pltpu.roll(head, 64, 1) * rots[1]).astype(bf16))
        return heads

    def row_scale():
        for k in range(1, 4):
            slot = ssb.at[lax.rem(t + 4 - k, 4)]
            remote(slot, slot, s_send.at[k - 1], s_recv.at[k - 1], sibling).wait_recv()
        squares = ssb[0, 0:1, :] + ssb[1, 0:1, :] + ssb[2, 0:1, :] + ssb[3, 0:1, :]
        scales.append(lax.rsqrt(to_column(squares) * (1.0 / WIDTH) + norm_eps))

    def key_mask():
        slot = pdb.at[1 - side]
        remote(slot, slot, d_send, d_recv, partner).wait_recv()
        key_pos = jnp.concatenate([pdb[0, 0:1, :], pdb[1, 0:1, :]], axis=1)
        key_doc = jnp.concatenate([pdb[0, 1:2, :], pdb[1, 1:2, :]], axis=1)
        masks.append((key_pos <= pos_col) & (key_doc == doc_col))

    scales, masks = [], []

    def share(j):
        rows = kvb.at[j, side]
        copy = remote(rows, rows, k_send.at[j], k_recv.at[j], partner)
        copy.start()
        sent.append(copy)

    def keys():
        first, second = rotated(summed(0))
        kvb[0, side, :, 0:HEAD] = first
        kvb[0, side, :, HEAD : 2 * HEAD] = second
        share(0)

    def values():
        kvb[1, side] = summed(1).astype(bf16)
        share(1)

    def attend(n):
        head = (n - 2) // 2
        queries = rotated(summed(n))
        key = kvb[0, :, :, head * HEAD : (head + 1) * HEAD].reshape(2 * KEPT, HEAD)
        value = kvb[1, :, :, head * HEAD : (head + 1) * HEAD].reshape(2 * KEPT, HEAD)
        for h in range(2):
            score = lax.dot_general(
                queries[h], key, (((1,), (1,)), ((), ())), preferred_element_type=f32
            ) * (HEAD ** -0.5)
            score = jnp.where(masks[0], score, -1e30)
            top = jnp.max(score, axis=1, keepdims=True)
            expo = jnp.exp(score - top)
            norm = jnp.sum(expo, axis=1, keepdims=True)
            mixed = jnp.dot(expo.astype(bf16), value, preferred_element_type=f32) / norm
            place_at = ((n - 2) * 2 + h) * HEAD
            out[:, place_at : place_at + HEAD] = mixed.astype(bf16)

    def joined():
        for j in range(2):
            slot = kvb.at[j, 1 - side]
            remote(slot, slot, k_send.at[j], k_recv.at[j], partner).wait_recv()

    def finish(n):
        (keys, values, attend)[min(n, 2)](*([n] if n >= 2 else []))

    steps = (
        (relay, 0, 1, 1), (relay, 0, 1, 0), (relay, 1, 1, 0), (relay, 1, 1, 1), (relay, 2, 1, 1),
        (relay, 2, 1, 0), (relay, 0, 2, 1), (relay, 0, 2, 0), (relay, 1, 2, 1), (relay, 1, 2, 0), (start, 3),
        (relay, 2, 2, 1), (relay, 2, 2, 0), (hand_on, 2), (relay, 0, 3, 0), (hand_on, 1), (relay, 1, 3, 1),
        (hand_on, 0), (hand_on, 3), (relay, 3, 1, 1), (relay, 3, 1, 0), (rows_ready,), (start, 4), (start, 5),
        (relay, 2, 3, 0), (product, 1), (product, 0), (relay, 3, 2, 0), (relay, 3, 2, 1), (relay, 4, 1, 1),
        (relay, 4, 1, 0), (relay, 5, 1, 1), (relay, 5, 1, 0), (second, 1, 2), (product, 2), (relay, 3, 3, 1),
        (second, 1, 1), (second, 0, 0), (second, 1, 3), (relay, 4, 2, 1), (relay, 4, 2, 0), (relay, 5, 2, 1),
        (relay, 5, 2, 0), (product, 3), (finish, 0), (relay, 4, 3, 0), (relay, 5, 3, 1), (second, 2, 0),
        (second, 3, 2), (second, 3, 1), (product, 4), (product, 5), (second, 3, 3), (finish, 1),
        (second, 5, 2), (second, 5, 1), (second, 4, 0), (second, 5, 3), (joined,), (finish, 2), (finish, 3),
        (finish, 4), (finish, 5),
    )
    for step in steps:
        step[0](*step[1:])
        if step[0] is rows_ready:
            row_scale()
            key_mask()
    for copy in sent:
        copy.wait_send()


def body(hidden, kept_index, doc_ids, norm_gain, w_query, key_value_weight):
    f32, bf16 = jnp.float32, jnp.bfloat16
    dma = pltpu.SemaphoreType.DMA
    vmem = pl.BlockSpec(memory_space=pltpu.VMEM)
    return pl.pallas_call(
        kernel,
        out_shape=jax.ShapeDtypeStruct((KEPT, 1024), bf16),
        in_specs=[pl.BlockSpec(memory_space=pl.ANY)] * 6,
        out_specs=vmem,
        scratch_shapes=[
            pltpu.VMEM((SPAN, QUARTER), bf16),
            pltpu.VMEM((1, KEPT), jnp.int32),
            pltpu.VMEM((1, SPAN), jnp.int32),
            pltpu.VMEM((16, 128), f32),
            pltpu.VMEM((128, 2, 256), bf16),
            pltpu.VMEM((8, KEPT, 256), bf16),
            pltpu.VMEM((4, 8, KEPT, 256), bf16),
            pltpu.VMEM((CHUNKS, 8, 128, CHUNK), bf16),
            pltpu.VMEM((CHUNKS, 8, KEPT, CHUNK), bf16),
            pltpu.VMEM((CHUNKS, 3, KEPT, CHUNK), bf16),
            pltpu.VMEM((CHUNKS, 7, KEPT, CHUNK), bf16),
            pltpu.VMEM((4, 8, 128), f32),
            pltpu.VMEM((2, 8, 128), f32),
            pltpu.VMEM((2, 2, KEPT, 256), bf16),
            pltpu.VMEM((2, KEPT, HEAD), f32),
            dma((9,)),
            dma((CHUNKS, 2, 4)), dma((CHUNKS, 2, 4)),
            dma((15,)), dma((15,)),
            dma((4,)), dma((4,)),
            dma((CHUNKS, 7)), dma((CHUNKS, 7)),
            dma((3,)), dma((3,)),
            dma, dma,
            dma((2,)), dma((2,)),
        ],
        compiler_params=pltpu.CompilerParams(
            collective_id=0, has_side_effects=True, vmem_limit_bytes=56 * 1024 * 1024
        ),
    )(
        hidden, kept_index, doc_ids.reshape(1, SPAN), norm_gain.reshape(WIDTH // 128, 128),
        w_query, key_value_weight,
    )


def solution(mesh):
    placed = (P("seq", "tp"), P("seq", None), P("seq"), P(), P("seq", "tp"), P("seq", None, "tp"))
    return jax.shard_map(
        body, mesh=mesh, in_specs=placed, out_specs=P("seq", "tp"), check_vma=False
    )
```

```python
import functools
import math

import jax
import jax.numpy as jnp
from jax import lax
from jax.experimental import pallas as pl
from jax.experimental.pallas import tpu as pltpu
from jax.sharding import PartitionSpec as P

MESH = pl.DeviceIdType.MESH
HEAD = 128
KEPT = 128
SPAN = 256
WIDTH = 8192
QUARTER = 2048
CHUNK = 256
CHUNKS = 6
norm_eps = 1e-05
rope_base = 10000.0

BEHIND = 40
X_FIRST = (True, False, True, True, False, True)


def kernel(
    hidden_in, kept_in, docs_in, gain_in, wq, wkv_in, out,
    hidden, kept, docs, gain, wkv, asrc, abuf, wbuf, pbuf, qbuf, rbuf, ssb, pdb, kvb, rots,
    load_sem, w_send, w_recv, a_send, a_recv, f_send, f_recv, p_send, p_recv,
    s_send, s_recv, d_send, d_recv, k_send, k_recv,
):
    f32, bf16 = jnp.float32, jnp.bfloat16
    s = lax.axis_index("seq")
    t = lax.axis_index("tp")
    z, xh, y = s // 8, lax.rem(s // 4, 2), lax.rem(s, 4)
    xl, c = t // 2, lax.rem(t, 2)
    x = xh * 2 + xl
    place = xh * 4 + y
    side = lax.rem(s, 2)

    def at(zz, xx, yy, cc):
        return (zz * 8 + (xx // 2) * 4 + yy, lax.rem(xx, 2) * 2 + cc)

    def plane(dx, dy):
        return lax.rem(x + dx + 4, 4), lax.rem(y + dy + 4, 4)

    up = (lax.rem(s + 8, 64), t)
    down = (lax.rem(s + 56, 64), t)
    sibling = (s, xl * 2 + (1 - c))
    partner = (s + 1 - 2 * side, t)
    moves = [(dx, dy) for dx in range(4) for dy in range(4) if (dx, dy) != (0, 0)]
    moves.sort(key=lambda m: -min(m[0], 4 - m[0]) - min(m[1], 4 - m[1]))

    loads = [
        pltpu.make_async_copy(src, dst, load_sem.at[i])
        for i, (src, dst) in enumerate(
            [
                (kept_in, kept),
                (docs_in, docs),
                (hidden_in, hidden),
                (gain_in.at[pl.ds(t * 16, 16)], gain),
                (wkv_in, wkv),
            ]
            + [(wq.at[:, pl.ds(n * CHUNK, CHUNK)], wbuf.at[n + 2, z]) for n in range(4)]
        )
    ]
    for load in loads:
        load.start()

    barrier = pltpu.get_barrier_semaphore()

    def greet(device):
        pl.semaphore_signal(barrier, inc=1, device_id=device, device_id_type=MESH)

    greet(up)
    greet(down)
    for dx, dy in moves:
        xx, yy = plane(dx, dy)
        greet(at(z, xx, yy, c))
    greet(sibling)
    greet((s, (1 - xl) * 2 + (1 - c)))

    for load in loads[4:]:
        load.wait()
    wbuf[0, z] = wkv[:, 0, :]
    wbuf[1, z] = wkv[:, 1, :]

    pl.semaphore_wait(barrier, 19)

    def remote(src, dst, send, recv, device):
        return pltpu.make_async_remote_copy(
            src_ref=src, dst_ref=dst, send_sem=send, recv_sem=recv, device_id=device, device_id_type=MESH
        )

    sent = []

    def hops(n, way):
        return 4 if (n + way) % 2 == 0 else 3

    def w_slot(n, way, hop):
        origin = lax.rem(z + 8 - hop, 8) if way == 0 else lax.rem(z + hop, 8)
        return wbuf.at[n, origin]

    def w_send_on(n, way, hop):
        slot = w_slot(n, way, hop - 1)
        copy = remote(slot, slot, w_send.at[n, way, hop - 1], w_recv.at[n, way, hop - 1], down if way else up)
        copy.start()
        sent.append(copy)

    def w_arrived(n, way, hop):
        slot = w_slot(n, way, hop)
        remote(slot, slot, w_send.at[n, way, hop - 1], w_recv.at[n, way, hop - 1], down if way else up).wait_recv()

    def start(n):
        for way in range(2):
            w_send_on(n, way, 1)

    def relay(n, hop, way):
        w_arrived(n, way, hop)
        w_send_on(n, way, hop + 1)

    for n in (0, 1, 2):
        start(n)

    lane = lax.broadcasted_iota(jnp.int32, (KEPT, KEPT), 1)
    eye = lax.broadcasted_iota(jnp.int32, (KEPT, KEPT), 0) == lane

    def to_column(row):
        return jnp.sum(jnp.where(eye, jnp.broadcast_to(row, (KEPT, KEPT)), 0.0), axis=1, keepdims=True)

    def to_row(column):
        return jnp.sum(jnp.where(eye, jnp.broadcast_to(column, (KEPT, KEPT)), 0.0), axis=0, keepdims=True)

    loads[0].wait()
    loads[1].wait()
    kept_row = kept[...].astype(f32)
    kept_col = to_column(kept_row)
    columns = lax.broadcasted_iota(jnp.int32, (KEPT, SPAN), 1).astype(f32)
    picks = columns == kept_col
    chosen = jnp.where(picks, 1.0, 0.0).astype(bf16)
    doc_col = jnp.sum(jnp.where(picks, docs[...].astype(f32), 0.0), axis=1, keepdims=True)
    pos_row = kept_row + (side * SPAN).astype(f32)
    pos_col = kept_col + (side * SPAN).astype(f32)
    pdb[side, 0:1, :] = pos_row
    pdb[side, 1:2, :] = to_row(doc_col)

    loads[2].wait()
    loads[3].wait()
    square = jnp.zeros((KEPT, 1), f32)
    for j in range(QUARTER // 256):
        rows = jnp.dot(chosen, hidden[:, j * 256 : (j + 1) * 256], preferred_element_type=f32)
        square += jnp.sum(rows * rows, axis=1, keepdims=True)
        for b in range(2):
            block = 2 * j + b
            scaled = rows[:, b * 128 : (b + 1) * 128] * gain[block : block + 1, :]
            high, to = block // 8, block % 8
            asrc[to, :, high * 128 : (high + 1) * 128] = scaled.astype(bf16)
    ssb[t, 0:1, :] = to_row(square)
    abuf[t, place] = asrc[place]

    for k, (dx, dy) in enumerate(moves):
        xx, yy = plane(dx, dy)
        copy = remote(asrc.at[(xx // 2) * 4 + yy], abuf.at[t, place], a_send.at[k], a_recv.at[k], at(z, xx, yy, c))
        copy.start()
        sent.append(copy)
    for k in range(1, 4):
        copy = remote(ssb.at[t], ssb.at[t], s_send.at[k - 1], s_recv.at[k - 1], (s, lax.rem(t + k, 4)))
        copy.start()
        sent.append(copy)
    copy = remote(pdb.at[side], pdb.at[side], d_send, d_recv, partner)
    copy.start()
    sent.append(copy)

    freqs = jnp.exp(lax.rem(lane, 64).astype(f32) * (-2.0 * math.log(rope_base) / HEAD))
    angles = pos_col * freqs
    rots[0] = jnp.cos(angles)
    sine = jnp.sin(angles)
    rots[1] = jnp.where(lane < 64, -sine, sine)

    def hand_on(dx):
        for dy in range(4):
            if (dx, dy) == (0, 0):
                continue
            k = moves.index((dx, dy))
            xx, yy = plane(-dx, -dy)
            slot = abuf.at[lax.rem(xx, 2) * 2 + c, (xx // 2) * 4 + yy]
            remote(slot, slot, a_send.at[k], a_recv.at[k], at(z, xx, yy, c)).wait_recv()
        xx, _ = plane(-dx, 0)
        block = abuf.at[lax.rem(xx, 2) * 2 + c, pl.ds((xx // 2) * 4, 4)]
        copy = remote(block, block, f_send.at[dx], f_recv.at[dx], sibling)
        copy.start()
        sent.append(copy)

    def rows_ready():
        for dx in range(4):
            xx, _ = plane(-dx, 0)
            block = abuf.at[lax.rem(xx, 2) * 2 + (1 - c), pl.ds((xx // 2) * 4, 4)]
            remote(block, block, f_send.at[dx], f_recv.at[dx], sibling).wait_recv()

    def product(n):
        for way in range(2):
            w_arrived(n, way, hops(n, way))

        def half(r):
            total = jnp.zeros((512, CHUNK), f32)
            for q in range(4):
                total += jnp.dot(
                    abuf[q, pl.ds(r * 4, 4)].reshape(512, 256),
                    wbuf[n, 2 * q : 2 * q + 2].reshape(256, CHUNK),
                    preferred_element_type=f32,
                )
            pbuf[n, pl.ds(r * 4, 4)] = total.astype(bf16).reshape(4, KEPT, CHUNK)

        pl.loop(0, 2)(half)
        for slot, block, device in first_step(n):
            copy = remote(pbuf.at[n, block], rbuf.at[n, slot], p_send.at[n, slot], p_recv.at[n, slot], device)
            copy.start()
            sent.append(copy)

    across = at(z, lax.rem(x + 2, 4), y, c)
    far_place = (1 - xh) * 4 + y

    def along(dy):
        return lax.rem(y + dy, 4)

    def first_step(n):
        if X_FIRST[n]:
            return [(dy, (1 - xh) * 4 + along(dy), across) for dy in (2, 1, 3, 0)]
        return [
            (3 * own + dy - 1, (xh if own else 1 - xh) * 4 + along(dy), at(z, x, along(dy), c))
            for own in range(2)
            for dy in (2, 1, 3)
        ]

    def arrived(n, slot):
        ref = rbuf.at[n, slot]
        remote(ref, ref, p_send.at[n, slot], p_recv.at[n, slot], across).wait_recv()
        return rbuf[n, slot].astype(f32)

    def second(n, dy):
        if X_FIRST[n]:
            total = pbuf[n, xh * 4 + along(dy)].astype(f32) + arrived(n, dy)
            slot, device = 3 + dy, at(z, x, along(dy), c)
        else:
            total = pbuf[n, far_place].astype(f32)
            for other in range(3):
                total += arrived(n, other)
            slot, device = 6, across
        qbuf[n, slot - 4] = total.astype(bf16)
        copy = remote(qbuf.at[n, slot - 4], rbuf.at[n, slot], p_send.at[n, slot], p_recv.at[n, slot], device)
        copy.start()
        sent.append(copy)

    def summed(n):
        total = pbuf[n, place].astype(f32)
        for slot in (0, 4, 6, 5) if X_FIRST[n] else (3, 5, 4, 6):
            total += arrived(n, slot)
        return total * scales[0]

    def rotated(block):
        heads = []
        for h in range(2):
            head = block[:, h * HEAD : (h + 1) * HEAD]
            heads.append((head * rots[0] + pltpu.roll(head, 64, 1) * rots[1]).astype(bf16))
        return heads

    def row_scale():
        for k in range(1, 4):
            slot = ssb.at[lax.rem(t + 4 - k, 4)]
            remote(slot, slot, s_send.at[k - 1], s_recv.at[k - 1], sibling).wait_recv()
        squares = ssb[0, 0:1, :] + ssb[1, 0:1, :] + ssb[2, 0:1, :] + ssb[3, 0:1, :]
        scales.append(lax.rsqrt(to_column(squares) * (1.0 / WIDTH) + norm_eps))

    def key_mask():
        slot = pdb.at[1 - side]
        remote(slot, slot, d_send, d_recv, partner).wait_recv()
        key_pos = jnp.concatenate([pdb[0, 0:1, :], pdb[1, 0:1, :]], axis=1)
        key_doc = jnp.concatenate([pdb[0, 1:2, :], pdb[1, 1:2, :]], axis=1)
        masks.append((key_pos <= pos_col) & (key_doc == doc_col))

    scales, masks = [], []

    def share(j):
        rows = kvb.at[j, side]
        copy = remote(rows, rows, k_send.at[j], k_recv.at[j], partner)
        copy.start()
        sent.append(copy)

    def keys():
        first, second = rotated(summed(0))
        kvb[0, side, :, 0:HEAD] = first
        kvb[0, side, :, HEAD : 2 * HEAD] = second
        share(0)

    def values():
        kvb[1, side] = summed(1).astype(bf16)
        share(1)

    def attend(n):
        head = (n - 2) // 2
        queries = rotated(summed(n))
        key = kvb[0, :, :, head * HEAD : (head + 1) * HEAD].reshape(2 * KEPT, HEAD)
        value = kvb[1, :, :, head * HEAD : (head + 1) * HEAD].reshape(2 * KEPT, HEAD)
        for h in range(2):
            score = lax.dot_general(
                queries[h], key, (((1,), (1,)), ((), ())), preferred_element_type=f32
            ) * (HEAD ** -0.5)
            score = jnp.where(masks[0], score, -1e30)
            top = jnp.max(score, axis=1, keepdims=True)
            expo = jnp.exp(score - top)
            norm = jnp.sum(expo, axis=1, keepdims=True)
            mixed = jnp.dot(expo.astype(bf16), value, preferred_element_type=f32) / norm
            place_at = ((n - 2) * 2 + h) * HEAD
            out[:, place_at : place_at + HEAD] = mixed.astype(bf16)

    def joined():
        for j in range(2):
            slot = kvb.at[j, 1 - side]
            remote(slot, slot, k_send.at[j], k_recv.at[j], partner).wait_recv()

    def finish(n):
        (keys, values, attend)[min(n, 2)](*([n] if n >= 2 else []))

    steps = (
        (relay, 0, 1, 0), (relay, 0, 1, 1), (relay, 1, 1, 0), (relay, 1, 1, 1), (relay, 2, 1, 1),
        (relay, 2, 1, 0), (relay, 0, 2, 0), (relay, 0, 2, 1), (relay, 1, 2, 1), (relay, 1, 2, 0),
        (relay, 2, 2, 1), (relay, 2, 2, 0), (hand_on, 2), (relay, 0, 3, 0), (hand_on, 1), (start, 3),
        (relay, 1, 3, 1), (start, 4), (start, 5), (hand_on, 3), (hand_on, 0), (relay, 2, 3, 0), (rows_ready,),
        (product, 0), (relay, 3, 1, 1), (relay, 3, 1, 0), (product, 1), (relay, 4, 1, 1), (relay, 4, 1, 0),
        (relay, 5, 1, 1), (relay, 5, 1, 0), (product, 2), (relay, 3, 2, 1), (relay, 3, 2, 0), (second, 0, 1),
        (second, 0, 2), (relay, 4, 2, 0), (relay, 4, 2, 1), (second, 0, 3), (second, 1, 0), (relay, 5, 2, 0),
        (relay, 5, 2, 1), (relay, 3, 3, 1), (second, 2, 2), (second, 2, 1), (relay, 4, 3, 0), (second, 2, 3),
        (relay, 5, 3, 1), (finish, 0), (product, 3), (product, 4), (finish, 1), (product, 5), (second, 4, 0),
        (second, 3, 3), (second, 3, 1), (second, 5, 2), (second, 3, 2), (joined,), (second, 5, 1),
        (finish, 2), (second, 5, 3), (finish, 4), (finish, 3), (finish, 5),
    )
    waited = 0
    for step in steps:
        while len(sent) - waited > BEHIND:
            sent[waited].wait_send()
            waited += 1
        step[0](*step[1:])
        if step[0] is rows_ready:
            row_scale()
            key_mask()
    for copy in sent[waited:]:
        copy.wait_send()


def body(hidden, kept_index, doc_ids, norm_gain, w_query, key_value_weight):
    f32, bf16 = jnp.float32, jnp.bfloat16
    dma = pltpu.SemaphoreType.DMA
    vmem = pl.BlockSpec(memory_space=pltpu.VMEM)
    return pl.pallas_call(
        kernel,
        out_shape=jax.ShapeDtypeStruct((KEPT, 1024), bf16),
        in_specs=[pl.BlockSpec(memory_space=pl.ANY)] * 6,
        out_specs=vmem,
        scratch_shapes=[
            pltpu.VMEM((SPAN, QUARTER), bf16),
            pltpu.VMEM((1, KEPT), jnp.int32),
            pltpu.VMEM((1, SPAN), jnp.int32),
            pltpu.VMEM((16, 128), f32),
            pltpu.VMEM((128, 2, 256), bf16),
            pltpu.VMEM((8, KEPT, 256), bf16),
            pltpu.VMEM((4, 8, KEPT, 256), bf16),
            pltpu.VMEM((CHUNKS, 8, 128, CHUNK), bf16),
            pltpu.VMEM((CHUNKS, 8, KEPT, CHUNK), bf16),
            pltpu.VMEM((CHUNKS, 3, KEPT, CHUNK), bf16),
            pltpu.VMEM((CHUNKS, 7, KEPT, CHUNK), bf16),
            pltpu.VMEM((4, 8, 128), f32),
            pltpu.VMEM((2, 8, 128), f32),
            pltpu.VMEM((2, 2, KEPT, 256), bf16),
            pltpu.VMEM((2, KEPT, HEAD), f32),
            dma((9,)),
            dma((CHUNKS, 2, 4)), dma((CHUNKS, 2, 4)),
            dma((15,)), dma((15,)),
            dma((4,)), dma((4,)),
            dma((CHUNKS, 7)), dma((CHUNKS, 7)),
            dma((3,)), dma((3,)),
            dma, dma,
            dma((2,)), dma((2,)),
        ],
        compiler_params=pltpu.CompilerParams(
            collective_id=0, has_side_effects=True, vmem_limit_bytes=56 * 1024 * 1024
        ),
    )(
        hidden, kept_index, doc_ids.reshape(1, SPAN), norm_gain.reshape(WIDTH // 128, 128),
        w_query, key_value_weight,
    )


def solution(mesh):
    placed = (P("seq", "tp"), P("seq", None), P("seq"), P(), P("seq", "tp"), P("seq", None, "tp"))
    return jax.shard_map(
        body, mesh=mesh, in_specs=placed, out_specs=P("seq", "tp"), check_vma=False
    )
```

```python
import functools
import math

import jax
import jax.numpy as jnp
from jax import lax
from jax.experimental import pallas as pl
from jax.experimental.pallas import tpu as pltpu
from jax.sharding import PartitionSpec as P

MESH = pl.DeviceIdType.MESH
HEAD = 128
KEPT = 128
SPAN = 256
WIDTH = 8192
QUARTER = 2048
CHUNK = 256
CHUNKS = 6
norm_eps = 1e-05
rope_base = 10000.0

BEHIND = 24
X_FIRST = (False, True, False, True, True, False)


def kernel(
    hidden_in, kept_in, docs_in, gain_in, wq, wkv_in, out,
    hidden, kept, docs, gain, wkv, asrc, abuf, wbuf, pbuf, qbuf, rbuf, ssb, pdb, kvb, rots,
    load_sem, w_send, w_recv, a_send, a_recv, f_send, f_recv, p_send, p_recv,
    s_send, s_recv, d_send, d_recv, k_send, k_recv,
):
    f32, bf16 = jnp.float32, jnp.bfloat16
    s = lax.axis_index("seq")
    t = lax.axis_index("tp")
    z, xh, y = s // 8, lax.rem(s // 4, 2), lax.rem(s, 4)
    xl, c = t // 2, lax.rem(t, 2)
    x = xh * 2 + xl
    place = xh * 4 + y
    side = lax.rem(s, 2)

    def at(zz, xx, yy, cc):
        return (zz * 8 + (xx // 2) * 4 + yy, lax.rem(xx, 2) * 2 + cc)

    def plane(dx, dy):
        return lax.rem(x + dx + 4, 4), lax.rem(y + dy + 4, 4)

    up = (lax.rem(s + 8, 64), t)
    down = (lax.rem(s + 56, 64), t)
    sibling = (s, xl * 2 + (1 - c))
    partner = (s + 1 - 2 * side, t)
    moves = [(dx, dy) for dx in range(4) for dy in range(4) if (dx, dy) != (0, 0)]
    moves.sort(key=lambda m: -min(m[0], 4 - m[0]) - min(m[1], 4 - m[1]))

    loads = [
        pltpu.make_async_copy(src, dst, load_sem.at[i])
        for i, (src, dst) in enumerate(
            [
                (kept_in, kept),
                (docs_in, docs),
                (hidden_in, hidden),
                (gain_in.at[pl.ds(t * 16, 16)], gain),
                (wkv_in, wkv),
            ]
            + [(wq.at[:, pl.ds(n * CHUNK, CHUNK)], wbuf.at[n + 2, z]) for n in range(4)]
        )
    ]
    for load in loads:
        load.start()

    barrier = pltpu.get_barrier_semaphore()

    def greet(device):
        pl.semaphore_signal(barrier, inc=1, device_id=device, device_id_type=MESH)

    greet(up)
    greet(down)
    for dx, dy in moves:
        xx, yy = plane(dx, dy)
        greet(at(z, xx, yy, c))
    greet(sibling)
    greet((s, (1 - xl) * 2 + (1 - c)))

    for load in loads[4:]:
        load.wait()
    wbuf[0, z] = wkv[:, 0, :]
    wbuf[1, z] = wkv[:, 1, :]

    pl.semaphore_wait(barrier, 19)

    def remote(src, dst, send, recv, device):
        return pltpu.make_async_remote_copy(
            src_ref=src, dst_ref=dst, send_sem=send, recv_sem=recv, device_id=device, device_id_type=MESH
        )

    sent = []

    def hops(n, way):
        return 4 if (n + way) % 2 == 0 else 3

    def w_slot(n, way, hop):
        origin = lax.rem(z + 8 - hop, 8) if way == 0 else lax.rem(z + hop, 8)
        return wbuf.at[n, origin]

    def w_send_on(n, way, hop):
        slot = w_slot(n, way, hop - 1)
        copy = remote(slot, slot, w_send.at[n, way, hop - 1], w_recv.at[n, way, hop - 1], down if way else up)
        copy.start()
        sent.append(copy)

    def w_arrived(n, way, hop):
        slot = w_slot(n, way, hop)
        remote(slot, slot, w_send.at[n, way, hop - 1], w_recv.at[n, way, hop - 1], down if way else up).wait_recv()

    def start(n):
        for way in range(2):
            w_send_on(n, way, 1)

    def relay(n, hop, way):
        w_arrived(n, way, hop)
        w_send_on(n, way, hop + 1)

    for n in (0, 1, 2):
        start(n)

    lane = lax.broadcasted_iota(jnp.int32, (KEPT, KEPT), 1)
    eye = lax.broadcasted_iota(jnp.int32, (KEPT, KEPT), 0) == lane

    def to_column(row):
        return jnp.sum(jnp.where(eye, jnp.broadcast_to(row, (KEPT, KEPT)), 0.0), axis=1, keepdims=True)

    def to_row(column):
        return jnp.sum(jnp.where(eye, jnp.broadcast_to(column, (KEPT, KEPT)), 0.0), axis=0, keepdims=True)

    loads[0].wait()
    loads[1].wait()
    kept_row = kept[...].astype(f32)
    kept_col = to_column(kept_row)
    columns = lax.broadcasted_iota(jnp.int32, (KEPT, SPAN), 1).astype(f32)
    picks = columns == kept_col
    chosen = jnp.where(picks, 1.0, 0.0).astype(bf16)
    doc_col = jnp.sum(jnp.where(picks, docs[...].astype(f32), 0.0), axis=1, keepdims=True)
    pos_row = kept_row + (side * SPAN).astype(f32)
    pos_col = kept_col + (side * SPAN).astype(f32)
    pdb[side, 0:1, :] = pos_row
    pdb[side, 1:2, :] = to_row(doc_col)

    loads[2].wait()
    loads[3].wait()
    square = jnp.zeros((KEPT, 1), f32)
    for j in range(QUARTER // 256):
        rows = jnp.dot(chosen, hidden[:, j * 256 : (j + 1) * 256], preferred_element_type=f32)
        square += jnp.sum(rows * rows, axis=1, keepdims=True)
        for b in range(2):
            block = 2 * j + b
            scaled = rows[:, b * 128 : (b + 1) * 128] * gain[block : block + 1, :]
            high, to = block // 8, block % 8
            asrc[to, :, high * 128 : (high + 1) * 128] = scaled.astype(bf16)
    ssb[t, 0:1, :] = to_row(square)
    abuf[t, place] = asrc[place]

    for k, (dx, dy) in enumerate(moves):
        xx, yy = plane(dx, dy)
        copy = remote(asrc.at[(xx // 2) * 4 + yy], abuf.at[t, place], a_send.at[k], a_recv.at[k], at(z, xx, yy, c))
        copy.start()
        sent.append(copy)
    for k in range(1, 4):
        copy = remote(ssb.at[t], ssb.at[t], s_send.at[k - 1], s_recv.at[k - 1], (s, lax.rem(t + k, 4)))
        copy.start()
        sent.append(copy)
    copy = remote(pdb.at[side], pdb.at[side], d_send, d_recv, partner)
    copy.start()
    sent.append(copy)

    freqs = jnp.exp(lax.rem(lane, 64).astype(f32) * (-2.0 * math.log(rope_base) / HEAD))
    angles = pos_col * freqs
    rots[0] = jnp.cos(angles)
    sine = jnp.sin(angles)
    rots[1] = jnp.where(lane < 64, -sine, sine)

    def hand_on(dx):
        for dy in range(4):
            if (dx, dy) == (0, 0):
                continue
            k = moves.index((dx, dy))
            xx, yy = plane(-dx, -dy)
            slot = abuf.at[lax.rem(xx, 2) * 2 + c, (xx // 2) * 4 + yy]
            remote(slot, slot, a_send.at[k], a_recv.at[k], at(z, xx, yy, c)).wait_recv()
        xx, _ = plane(-dx, 0)
        block = abuf.at[lax.rem(xx, 2) * 2 + c, pl.ds((xx // 2) * 4, 4)]
        copy = remote(block, block, f_send.at[dx], f_recv.at[dx], sibling)
        copy.start()
        sent.append(copy)

    def rows_ready():
        for dx in range(4):
            xx, _ = plane(-dx, 0)
            block = abuf.at[lax.rem(xx, 2) * 2 + (1 - c), pl.ds((xx // 2) * 4, 4)]
            remote(block, block, f_send.at[dx], f_recv.at[dx], sibling).wait_recv()

    def product(n):
        for way in range(2):
            w_arrived(n, way, hops(n, way))

        def half(r):
            total = jnp.zeros((512, CHUNK), f32)
            for q in range(4):
                total += jnp.dot(
                    abuf[q, pl.ds(r * 4, 4)].reshape(512, 256),
                    wbuf[n, 2 * q : 2 * q + 2].reshape(256, CHUNK),
                    preferred_element_type=f32,
                )
            pbuf[n, pl.ds(r * 4, 4)] = total.astype(bf16).reshape(4, KEPT, CHUNK)

        pl.loop(0, 2)(half)
        for slot, block, device in first_step(n):
            copy = remote(pbuf.at[n, block], rbuf.at[n, slot], p_send.at[n, slot], p_recv.at[n, slot], device)
            copy.start()
            sent.append(copy)

    across = at(z, lax.rem(x + 2, 4), y, c)
    far_place = (1 - xh) * 4 + y

    def along(dy):
        return lax.rem(y + dy, 4)

    def first_step(n):
        if X_FIRST[n]:
            return [(dy, (1 - xh) * 4 + along(dy), across) for dy in (2, 1, 3, 0)]
        return [
            (3 * own + dy - 1, (xh if own else 1 - xh) * 4 + along(dy), at(z, x, along(dy), c))
            for own in range(2)
            for dy in (2, 1, 3)
        ]

    def arrived(n, slot):
        ref = rbuf.at[n, slot]
        remote(ref, ref, p_send.at[n, slot], p_recv.at[n, slot], across).wait_recv()
        return rbuf[n, slot].astype(f32)

    def second(n, dy):
        if X_FIRST[n]:
            total = pbuf[n, xh * 4 + along(dy)].astype(f32) + arrived(n, dy)
            slot, device = 3 + dy, at(z, x, along(dy), c)
        else:
            total = pbuf[n, far_place].astype(f32)
            for other in range(3):
                total += arrived(n, other)
            slot, device = 6, across
        qbuf[n, slot - 4] = total.astype(bf16)
        copy = remote(qbuf.at[n, slot - 4], rbuf.at[n, slot], p_send.at[n, slot], p_recv.at[n, slot], device)
        copy.start()
        sent.append(copy)

    def summed(n):
        total = pbuf[n, place].astype(f32)
        for slot in (0, 4, 6, 5) if X_FIRST[n] else (3, 5, 4, 6):
            total += arrived(n, slot)
        return total * scales[0]

    def rotated(block):
        heads = []
        for h in range(2):
            head = block[:, h * HEAD : (h + 1) * HEAD]
            heads.append((head * rots[0] + pltpu.roll(head, 64, 1) * rots[1]).astype(bf16))
        return heads

    def row_scale():
        for k in range(1, 4):
            slot = ssb.at[lax.rem(t + 4 - k, 4)]
            remote(slot, slot, s_send.at[k - 1], s_recv.at[k - 1], sibling).wait_recv()
        squares = ssb[0, 0:1, :] + ssb[1, 0:1, :] + ssb[2, 0:1, :] + ssb[3, 0:1, :]
        scales.append(lax.rsqrt(to_column(squares) * (1.0 / WIDTH) + norm_eps))

    def key_mask():
        slot = pdb.at[1 - side]
        remote(slot, slot, d_send, d_recv, partner).wait_recv()
        key_pos = jnp.concatenate([pdb[0, 0:1, :], pdb[1, 0:1, :]], axis=1)
        key_doc = jnp.concatenate([pdb[0, 1:2, :], pdb[1, 1:2, :]], axis=1)
        masks.append((key_pos <= pos_col) & (key_doc == doc_col))

    scales, masks = [], []

    def share(j):
        rows = kvb.at[j, side]
        copy = remote(rows, rows, k_send.at[j], k_recv.at[j], partner)
        copy.start()
        sent.append(copy)

    def keys():
        first, second = rotated(summed(0))
        kvb[0, side, :, 0:HEAD] = first
        kvb[0, side, :, HEAD : 2 * HEAD] = second
        share(0)

    def values():
        kvb[1, side] = summed(1).astype(bf16)
        share(1)

    def attend(n):
        head = (n - 2) // 2
        queries = rotated(summed(n))
        key = kvb[0, :, :, head * HEAD : (head + 1) * HEAD].reshape(2 * KEPT, HEAD)
        value = kvb[1, :, :, head * HEAD : (head + 1) * HEAD].reshape(2 * KEPT, HEAD)
        for h in range(2):
            score = lax.dot_general(
                queries[h], key, (((1,), (1,)), ((), ())), preferred_element_type=f32
            ) * (HEAD ** -0.5)
            score = jnp.where(masks[0], score, -1e30)
            top = jnp.max(score, axis=1, keepdims=True)
            expo = jnp.exp(score - top)
            norm = jnp.sum(expo, axis=1, keepdims=True)
            mixed = jnp.dot(expo.astype(bf16), value, preferred_element_type=f32) / norm
            place_at = ((n - 2) * 2 + h) * HEAD
            out[:, place_at : place_at + HEAD] = mixed.astype(bf16)

    def joined():
        for j in range(2):
            slot = kvb.at[j, 1 - side]
            remote(slot, slot, k_send.at[j], k_recv.at[j], partner).wait_recv()

    def finish(n):
        (keys, values, attend)[min(n, 2)](*([n] if n >= 2 else []))

    steps = (
        (relay, 0, 1, 0), (relay, 0, 1, 1), (relay, 1, 1, 1), (relay, 1, 1, 0), (relay, 2, 1, 1),
        (relay, 2, 1, 0), (relay, 0, 2, 0), (relay, 0, 2, 1), (relay, 1, 2, 1), (relay, 1, 2, 0),
        (relay, 2, 2, 1), (relay, 2, 2, 0), (relay, 0, 3, 0), (start, 3), (hand_on, 2), (hand_on, 1),
        (relay, 1, 3, 1), (start, 4), (hand_on, 3), (hand_on, 0), (start, 5), (rows_ready,), (product, 0),
        (relay, 2, 3, 0), (relay, 3, 1, 1), (relay, 3, 1, 0), (product, 1), (relay, 4, 1, 1),
        (relay, 4, 1, 0), (relay, 5, 1, 1), (relay, 5, 1, 0), (product, 2), (relay, 3, 2, 1),
        (relay, 3, 2, 0), (second, 1, 2), (relay, 4, 2, 1), (relay, 4, 2, 0), (second, 0, 0),
        (relay, 5, 2, 1), (relay, 5, 2, 0), (second, 1, 1), (second, 1, 3), (relay, 3, 3, 1), (second, 2, 0),
        (relay, 4, 3, 0), (finish, 0), (relay, 5, 3, 1), (product, 3), (product, 4), (finish, 1),
        (product, 5), (second, 3, 2), (joined,), (second, 3, 1), (second, 5, 0), (second, 3, 3), (finish, 2),
        (second, 4, 2), (second, 4, 1), (second, 4, 3), (finish, 3), (finish, 5), (finish, 4),
    )
    waited = 0
    for step in steps:
        while len(sent) - waited > BEHIND:
            sent[waited].wait_send()
            waited += 1
        step[0](*step[1:])
        if step[0] is rows_ready:
            row_scale()
            key_mask()
    for copy in sent[waited:]:
        copy.wait_send()


def body(hidden, kept_index, doc_ids, norm_gain, w_query, key_value_weight):
    f32, bf16 = jnp.float32, jnp.bfloat16
    dma = pltpu.SemaphoreType.DMA
    vmem = pl.BlockSpec(memory_space=pltpu.VMEM)
    return pl.pallas_call(
        kernel,
        out_shape=jax.ShapeDtypeStruct((KEPT, 1024), bf16),
        in_specs=[pl.BlockSpec(memory_space=pl.ANY)] * 6,
        out_specs=vmem,
        scratch_shapes=[
            pltpu.VMEM((SPAN, QUARTER), bf16),
            pltpu.VMEM((1, KEPT), jnp.int32),
            pltpu.VMEM((1, SPAN), jnp.int32),
            pltpu.VMEM((16, 128), f32),
            pltpu.VMEM((128, 2, 256), bf16),
            pltpu.VMEM((8, KEPT, 256), bf16),
            pltpu.VMEM((4, 8, KEPT, 256), bf16),
            pltpu.VMEM((CHUNKS, 8, 128, CHUNK), bf16),
            pltpu.VMEM((CHUNKS, 8, KEPT, CHUNK), bf16),
            pltpu.VMEM((CHUNKS, 3, KEPT, CHUNK), bf16),
            pltpu.VMEM((CHUNKS, 7, KEPT, CHUNK), bf16),
            pltpu.VMEM((4, 8, 128), f32),
            pltpu.VMEM((2, 8, 128), f32),
            pltpu.VMEM((2, 2, KEPT, 256), bf16),
            pltpu.VMEM((2, KEPT, HEAD), f32),
            dma((9,)),
            dma((CHUNKS, 2, 4)), dma((CHUNKS, 2, 4)),
            dma((15,)), dma((15,)),
            dma((4,)), dma((4,)),
            dma((CHUNKS, 7)), dma((CHUNKS, 7)),
            dma((3,)), dma((3,)),
            dma, dma,
            dma((2,)), dma((2,)),
        ],
        compiler_params=pltpu.CompilerParams(
            collective_id=0, has_side_effects=True, vmem_limit_bytes=56 * 1024 * 1024
        ),
    )(
        hidden, kept_index, doc_ids.reshape(1, SPAN), norm_gain.reshape(WIDTH // 128, 128),
        w_query, key_value_weight,
    )


def solution(mesh):
    placed = (P("seq", "tp"), P("seq", None), P("seq"), P(), P("seq", "tp"), P("seq", None, "tp"))
    return jax.shard_map(
        body, mesh=mesh, in_specs=placed, out_specs=P("seq", "tp"), check_vma=False
    )
```

```python
import functools
import math

import jax
import jax.numpy as jnp
from jax import lax
from jax.experimental import pallas as pl
from jax.experimental.pallas import tpu as pltpu
from jax.sharding import PartitionSpec as P

MESH = pl.DeviceIdType.MESH
HEAD = 128
KEPT = 128
SPAN = 256
WIDTH = 8192
QUARTER = 2048
CHUNK = 256
CHUNKS = 6
norm_eps = 1e-05
rope_base = 10000.0

BEHIND = 24
X_FIRST = (False, True, False, True, True, False)


def kernel(
    hidden_in, kept_in, docs_in, gain_in, wq, wkv_in, out,
    hidden, kept, docs, gain, wkv, asrc, abuf, wbuf, pbuf, qbuf, rbuf, ssb, pdb, kvb, rots,
    load_sem, w_send, w_recv, a_send, a_recv, f_send, f_recv, p_send, p_recv,
    s_send, s_recv, d_send, d_recv, k_send, k_recv,
):
    f32, bf16 = jnp.float32, jnp.bfloat16
    s = lax.axis_index("seq")
    t = lax.axis_index("tp")
    z, xh, y = s // 8, lax.rem(s // 4, 2), lax.rem(s, 4)
    xl, c = t // 2, lax.rem(t, 2)
    x = xh * 2 + xl
    place = xh * 4 + y
    side = lax.rem(s, 2)

    def at(zz, xx, yy, cc):
        return (zz * 8 + (xx // 2) * 4 + yy, lax.rem(xx, 2) * 2 + cc)

    def plane(dx, dy):
        return lax.rem(x + dx + 4, 4), lax.rem(y + dy + 4, 4)

    up = (lax.rem(s + 8, 64), t)
    down = (lax.rem(s + 56, 64), t)
    sibling = (s, xl * 2 + (1 - c))
    partner = (s + 1 - 2 * side, t)
    moves = [(dx, dy) for dx in range(4) for dy in range(4) if (dx, dy) != (0, 0)]
    moves.sort(key=lambda m: -min(m[0], 4 - m[0]) - min(m[1], 4 - m[1]))

    loads = [
        pltpu.make_async_copy(src, dst, load_sem.at[i])
        for i, (src, dst) in enumerate(
            [
                (kept_in, kept),
                (docs_in, docs),
                (hidden_in, hidden),
                (gain_in.at[pl.ds(t * 16, 16)], gain),
                (wkv_in, wkv),
            ]
            + [(wq.at[:, pl.ds(n * CHUNK, CHUNK)], wbuf.at[n + 2, z]) for n in range(4)]
        )
    ]
    for load in loads:
        load.start()

    barrier = pltpu.get_barrier_semaphore()

    def greet(device):
        pl.semaphore_signal(barrier, inc=1, device_id=device, device_id_type=MESH)

    greet(up)
    greet(down)
    for dx, dy in moves:
        xx, yy = plane(dx, dy)
        greet(at(z, xx, yy, c))
    greet(sibling)
    greet((s, (1 - xl) * 2 + (1 - c)))

    for load in loads[4:]:
        load.wait()
    wbuf[0, z] = wkv[:, 0, :]
    wbuf[1, z] = wkv[:, 1, :]

    pl.semaphore_wait(barrier, 19)

    def remote(src, dst, send, recv, device):
        return pltpu.make_async_remote_copy(
            src_ref=src, dst_ref=dst, send_sem=send, recv_sem=recv, device_id=device, device_id_type=MESH
        )

    sent = []

    def hops(n, way):
        return 4 if (n + way) % 2 == 0 else 3

    def w_slot(n, way, hop):
        origin = lax.rem(z + 8 - hop, 8) if way == 0 else lax.rem(z + hop, 8)
        return wbuf.at[n, origin]

    def w_send_on(n, way, hop):
        slot = w_slot(n, way, hop - 1)
        copy = remote(slot, slot, w_send.at[n, way, hop - 1], w_recv.at[n, way, hop - 1], down if way else up)
        copy.start()
        sent.append(copy)

    def w_arrived(n, way, hop):
        slot = w_slot(n, way, hop)
        remote(slot, slot, w_send.at[n, way, hop - 1], w_recv.at[n, way, hop - 1], down if way else up).wait_recv()

    def start(n):
        for way in range(2):
            w_send_on(n, way, 1)

    def relay(n, hop, way):
        w_arrived(n, way, hop)
        w_send_on(n, way, hop + 1)

    for n in (0, 1, 2):
        start(n)

    lane = lax.broadcasted_iota(jnp.int32, (KEPT, KEPT), 1)
    eye = lax.broadcasted_iota(jnp.int32, (KEPT, KEPT), 0) == lane

    def to_column(row):
        return jnp.sum(jnp.where(eye, jnp.broadcast_to(row, (KEPT, KEPT)), 0.0), axis=1, keepdims=True)

    def to_row(column):
        return jnp.sum(jnp.where(eye, jnp.broadcast_to(column, (KEPT, KEPT)), 0.0), axis=0, keepdims=True)

    loads[0].wait()
    loads[1].wait()
    kept_row = kept[...].astype(f32)
    kept_col = to_column(kept_row)
    columns = lax.broadcasted_iota(jnp.int32, (KEPT, SPAN), 1).astype(f32)
    picks = columns == kept_col
    chosen = jnp.where(picks, 1.0, 0.0).astype(bf16)
    doc_col = jnp.sum(jnp.where(picks, docs[...].astype(f32), 0.0), axis=1, keepdims=True)
    pos_row = kept_row + (side * SPAN).astype(f32)
    pos_col = kept_col + (side * SPAN).astype(f32)
    pdb[side, 0:1, :] = pos_row
    pdb[side, 1:2, :] = to_row(doc_col)

    loads[2].wait()
    loads[3].wait()
    square = jnp.zeros((KEPT, 1), f32)
    for j in range(QUARTER // 256):
        rows = jnp.dot(chosen, hidden[:, j * 256 : (j + 1) * 256], preferred_element_type=f32)
        square += jnp.sum(rows * rows, axis=1, keepdims=True)
        for b in range(2):
            block = 2 * j + b
            scaled = rows[:, b * 128 : (b + 1) * 128] * gain[block : block + 1, :]
            high, to = block // 8, block % 8
            asrc[to, :, high * 128 : (high + 1) * 128] = scaled.astype(bf16)
    ssb[t, 0:1, :] = to_row(square)
    abuf[t, place] = asrc[place]

    for k, (dx, dy) in enumerate(moves):
        xx, yy = plane(dx, dy)
        copy = remote(asrc.at[(xx // 2) * 4 + yy], abuf.at[t, place], a_send.at[k], a_recv.at[k], at(z, xx, yy, c))
        copy.start()
        sent.append(copy)
    for k in range(1, 4):
        copy = remote(ssb.at[t], ssb.at[t], s_send.at[k - 1], s_recv.at[k - 1], (s, lax.rem(t + k, 4)))
        copy.start()
        sent.append(copy)
    copy = remote(pdb.at[side], pdb.at[side], d_send, d_recv, partner)
    copy.start()
    sent.append(copy)

    freqs = jnp.exp(lax.rem(lane, 64).astype(f32) * (-2.0 * math.log(rope_base) / HEAD))
    angles = pos_col * freqs
    rots[0] = jnp.cos(angles)
    sine = jnp.sin(angles)
    rots[1] = jnp.where(lane < 64, -sine, sine)

    def hand_on(dx):
        for dy in range(4):
            if (dx, dy) == (0, 0):
                continue
            k = moves.index((dx, dy))
            xx, yy = plane(-dx, -dy)
            slot = abuf.at[lax.rem(xx, 2) * 2 + c, (xx // 2) * 4 + yy]
            remote(slot, slot, a_send.at[k], a_recv.at[k], at(z, xx, yy, c)).wait_recv()
        xx, _ = plane(-dx, 0)
        block = abuf.at[lax.rem(xx, 2) * 2 + c, pl.ds((xx // 2) * 4, 4)]
        copy = remote(block, block, f_send.at[dx], f_recv.at[dx], sibling)
        copy.start()
        sent.append(copy)

    def rows_ready():
        for dx in range(4):
            xx, _ = plane(-dx, 0)
            block = abuf.at[lax.rem(xx, 2) * 2 + (1 - c), pl.ds((xx // 2) * 4, 4)]
            remote(block, block, f_send.at[dx], f_recv.at[dx], sibling).wait_recv()

    def product(n):
        for way in range(2):
            w_arrived(n, way, hops(n, way))

        def half(r):
            total = jnp.zeros((512, CHUNK), f32)
            for q in range(4):
                total += jnp.dot(
                    abuf[q, pl.ds(r * 4, 4)].reshape(512, 256),
                    wbuf[n, 2 * q : 2 * q + 2].reshape(256, CHUNK),
                    preferred_element_type=f32,
                )
            pbuf[n, pl.ds(r * 4, 4)] = total.astype(bf16).reshape(4, KEPT, CHUNK)

        steps_out = first_step(n)
        far = 4 if X_FIRST[n] else 3
        for r, group in ((1 - xh, steps_out[:far]), (xh, steps_out[far:])):
            half(r)
            for slot, block, device in group:
                copy = remote(pbuf.at[n, block], rbuf.at[n, slot], p_send.at[n, slot], p_recv.at[n, slot], device)
                copy.start()
                sent.append(copy)

    across = at(z, lax.rem(x + 2, 4), y, c)
    far_place = (1 - xh) * 4 + y

    def along(dy):
        return lax.rem(y + dy, 4)

    def first_step(n):
        if X_FIRST[n]:
            return [(dy, (1 - xh) * 4 + along(dy), across) for dy in (2, 1, 3, 0)]
        return [
            (3 * own + dy - 1, (xh if own else 1 - xh) * 4 + along(dy), at(z, x, along(dy), c))
            for own in range(2)
            for dy in (2, 1, 3)
        ]

    def arrived(n, slot):
        ref = rbuf.at[n, slot]
        remote(ref, ref, p_send.at[n, slot], p_recv.at[n, slot], across).wait_recv()
        return rbuf[n, slot].astype(f32)

    def second(n, dy):
        if X_FIRST[n]:
            total = pbuf[n, xh * 4 + along(dy)].astype(f32) + arrived(n, dy)
            slot, device = 3 + dy, at(z, x, along(dy), c)
        else:
            total = pbuf[n, far_place].astype(f32)
            for other in range(3):
                total += arrived(n, other)
            slot, device = 6, across
        qbuf[n, slot - 4] = total.astype(bf16)
        copy = remote(qbuf.at[n, slot - 4], rbuf.at[n, slot], p_send.at[n, slot], p_recv.at[n, slot], device)
        copy.start()
        sent.append(copy)

    def summed(n):
        total = pbuf[n, place].astype(f32)
        for slot in (0, 4, 6, 5) if X_FIRST[n] else (3, 5, 4, 6):
            total += arrived(n, slot)
        return total * scales[0]

    def rotated(block):
        heads = []
        for h in range(2):
            head = block[:, h * HEAD : (h + 1) * HEAD]
            heads.append((head * rots[0] + pltpu.roll(head, 64, 1) * rots[1]).astype(bf16))
        return heads

    def row_scale():
        for k in range(1, 4):
            slot = ssb.at[lax.rem(t + 4 - k, 4)]
            remote(slot, slot, s_send.at[k - 1], s_recv.at[k - 1], sibling).wait_recv()
        squares = ssb[0, 0:1, :] + ssb[1, 0:1, :] + ssb[2, 0:1, :] + ssb[3, 0:1, :]
        scales.append(lax.rsqrt(to_column(squares) * (1.0 / WIDTH) + norm_eps))

    def key_mask():
        slot = pdb.at[1 - side]
        remote(slot, slot, d_send, d_recv, partner).wait_recv()
        key_pos = jnp.concatenate([pdb[0, 0:1, :], pdb[1, 0:1, :]], axis=1)
        key_doc = jnp.concatenate([pdb[0, 1:2, :], pdb[1, 1:2, :]], axis=1)
        masks.append((key_pos <= pos_col) & (key_doc == doc_col))

    scales, masks = [], []

    def share(j):
        rows = kvb.at[j, side]
        copy = remote(rows, rows, k_send.at[j], k_recv.at[j], partner)
        copy.start()
        sent.append(copy)

    def keys():
        first, second = rotated(summed(0))
        kvb[0, side, :, 0:HEAD] = first
        kvb[0, side, :, HEAD : 2 * HEAD] = second
        share(0)

    def values():
        kvb[1, side] = summed(1).astype(bf16)
        share(1)

    def attend(n):
        head = (n - 2) // 2
        queries = rotated(summed(n))
        key = kvb[0, :, :, head * HEAD : (head + 1) * HEAD].reshape(2 * KEPT, HEAD)
        value = kvb[1, :, :, head * HEAD : (head + 1) * HEAD].reshape(2 * KEPT, HEAD)
        for h in range(2):
            score = lax.dot_general(
                queries[h], key, (((1,), (1,)), ((), ())), preferred_element_type=f32
            ) * (HEAD ** -0.5)
            score = jnp.where(masks[0], score, -1e30)
            top = jnp.max(score, axis=1, keepdims=True)
            expo = jnp.exp(score - top)
            norm = jnp.sum(expo, axis=1, keepdims=True)
            mixed = jnp.dot(expo.astype(bf16), value, preferred_element_type=f32) / norm
            place_at = ((n - 2) * 2 + h) * HEAD
            out[:, place_at : place_at + HEAD] = mixed.astype(bf16)

    def joined():
        for j in range(2):
            slot = kvb.at[j, 1 - side]
            remote(slot, slot, k_send.at[j], k_recv.at[j], partner).wait_recv()

    def finish(n):
        (keys, values, attend)[min(n, 2)](*([n] if n >= 2 else []))

    steps = (
        (relay, 0, 1, 0), (relay, 0, 1, 1), (relay, 1, 1, 1), (relay, 1, 1, 0), (relay, 2, 1, 1),
        (relay, 2, 1, 0), (relay, 0, 2, 0), (relay, 0, 2, 1), (relay, 1, 2, 1), (relay, 1, 2, 0),
        (relay, 2, 2, 1), (relay, 2, 2, 0), (relay, 0, 3, 0), (start, 3), (hand_on, 2), (hand_on, 1),
        (relay, 1, 3, 1), (start, 4), (hand_on, 3), (hand_on, 0), (start, 5), (rows_ready,), (product, 0),
        (relay, 2, 3, 0), (relay, 3, 1, 1), (relay, 3, 1, 0), (product, 1), (relay, 4, 1, 1),
        (relay, 4, 1, 0), (relay, 5, 1, 1), (relay, 5, 1, 0), (product, 2), (relay, 3, 2, 1),
        (relay, 3, 2, 0), (second, 1, 2), (relay, 4, 2, 1), (relay, 4, 2, 0), (second, 0, 0),
        (relay, 5, 2, 1), (relay, 5, 2, 0), (second, 1, 1), (second, 1, 3), (relay, 3, 3, 1), (second, 2, 0),
        (relay, 4, 3, 0), (finish, 0), (relay, 5, 3, 1), (product, 3), (product, 4), (finish, 1),
        (product, 5), (second, 3, 2), (joined,), (second, 3, 1), (second, 5, 0), (second, 3, 3), (finish, 2),
        (second, 4, 2), (second, 4, 1), (second, 4, 3), (finish, 3), (finish, 5), (finish, 4),
    )
    waited = 0
    for step in steps:
        while len(sent) - waited > BEHIND:
            sent[waited].wait_send()
            waited += 1
        step[0](*step[1:])
        if step[0] is rows_ready:
            row_scale()
            key_mask()
    for copy in sent[waited:]:
        copy.wait_send()


def body(hidden, kept_index, doc_ids, norm_gain, w_query, key_value_weight):
    f32, bf16 = jnp.float32, jnp.bfloat16
    dma = pltpu.SemaphoreType.DMA
    vmem = pl.BlockSpec(memory_space=pltpu.VMEM)
    return pl.pallas_call(
        kernel,
        out_shape=jax.ShapeDtypeStruct((KEPT, 1024), bf16),
        in_specs=[pl.BlockSpec(memory_space=pl.ANY)] * 6,
        out_specs=vmem,
        scratch_shapes=[
            pltpu.VMEM((SPAN, QUARTER), bf16),
            pltpu.VMEM((1, KEPT), jnp.int32),
            pltpu.VMEM((1, SPAN), jnp.int32),
            pltpu.VMEM((16, 128), f32),
            pltpu.VMEM((128, 2, 256), bf16),
            pltpu.VMEM((8, KEPT, 256), bf16),
            pltpu.VMEM((4, 8, KEPT, 256), bf16),
            pltpu.VMEM((CHUNKS, 8, 128, CHUNK), bf16),
            pltpu.VMEM((CHUNKS, 8, KEPT, CHUNK), bf16),
            pltpu.VMEM((CHUNKS, 3, KEPT, CHUNK), bf16),
            pltpu.VMEM((CHUNKS, 7, KEPT, CHUNK), bf16),
            pltpu.VMEM((4, 8, 128), f32),
            pltpu.VMEM((2, 8, 128), f32),
            pltpu.VMEM((2, 2, KEPT, 256), bf16),
            pltpu.VMEM((2, KEPT, HEAD), f32),
            dma((9,)),
            dma((CHUNKS, 2, 4)), dma((CHUNKS, 2, 4)),
            dma((15,)), dma((15,)),
            dma((4,)), dma((4,)),
            dma((CHUNKS, 7)), dma((CHUNKS, 7)),
            dma((3,)), dma((3,)),
            dma, dma,
            dma((2,)), dma((2,)),
        ],
        compiler_params=pltpu.CompilerParams(
            collective_id=0, has_side_effects=True, vmem_limit_bytes=56 * 1024 * 1024
        ),
    )(
        hidden, kept_index, doc_ids.reshape(1, SPAN), norm_gain.reshape(WIDTH // 128, 128),
        w_query, key_value_weight,
    )


def solution(mesh):
    placed = (P("seq", "tp"), P("seq", None), P("seq"), P(), P("seq", "tp"), P("seq", None, "tp"))
    return jax.shard_map(
        body, mesh=mesh, in_specs=placed, out_specs=P("seq", "tp"), check_vma=False
    )
```
